256 devices in a mesh: dp: 2 (over x_hi), ctx: 16 (over z, core), tp: 8 (over x_lo, y).
Axes of the slice: x: 4 (x_hi: 2, x_lo: 2; x = x_hi * 2 + x_lo), y: 4, z: 8, core: 2. Of those that a mesh axis runs over, the one named last changes fastest.
Arguments:
- tokens: bfloat16 [8192, 3072], P(('dp', 'ctx'), 'tp'), parts along dimension 0, may hold values from -20 to 20
- tangent: bfloat16 [8192, 3072], P(('dp', 'ctx'), 'tp'), parts along dimension 0, may hold values from -6 to 6
- w_query: bfloat16 [3072, 3072], P(None, 'tp'), may hold values from -0.109375 to 0.109375
- w_key: bfloat16 [3072, 3072], P(None, 'tp'), may hold values from -0.109375 to 0.109375
- w_value: bfloat16 [3072, 3072], P(None, 'tp'), may hold values from -0.109375 to 0.109375
- w_output: bfloat16 [3072, 3072], P('tp'), may hold values from -0.4375 to 0.4375
Outputs:
- layer_out: bfloat16 [8192, 3072], P(('dp', 'ctx'), 'tp'), parts along dimension 0
- layer_tangent: bfloat16 [8192, 3072], P(('dp', 'ctx'), 'tp'), parts along dimension 0
The draws below stay inside these ranges and needn't reach their ends.
There are 2 independent parts, one for each index of `dp`. The reference program is written for one: setup_inputs(seed, part) draws one part's arguments, and reference() takes and returns one part's arrays. A program takes and returns all parts, laid end to end along the dimension named above; an argument that names none is the same for every part. Nothing has to cross between parts.
All inputs are finite; a program needn't handle non-finite values.
Results may differ from the reference program's by a relative error of at most 0.02.
The reference program's roundings to bfloat16 on the way count: a program that leaves them out, or rounds other values in their place, can miss the bound.
Values may be sent and summed in bfloat16 or wider, within the bound.
A program may use at most 128 MiB of HBM per device.

```python
import math
import jax
import jax.numpy as jnp
from jax import lax

HEADS = 24
HEAD_DIM = 128
D = 3072
TOKENS = 4096


def draw_tokens(key, part):
    key = jax.random.fold_in(key, 11)
    base = jax.random.truncated_normal(key, -6.0, 6.0, (TOKENS, D), jnp.float32)
    return (1.4 * base).astype(jnp.bfloat16)


def shard_levels(stream_key, dims, shards, least, top_value):
    factor_of = 1.0
    for position, shards_of in shards:
        heights = jax.random.uniform(jax.random.fold_in(jax.random.fold_in(stream_key, 6), position), (shards_of,), jnp.float32, least / len(shards), top_value / len(shards))
        factor_of = factor_of * jnp.repeat(jnp.exp(heights), dims[position] // shards_of).reshape((-1,) + (1,) * (len(dims) - 1 - position))
    return factor_of


def centred(rng, shape, width, reach, shards=(), held_as=jnp.bfloat16):
    drawn = jax.random.normal(rng, shape, jnp.float32) * width
    if len(shards) > 0:
        drawn = shard_levels(rng, shape, shards, -0.22, 0.18) * drawn
    return jnp.clip(drawn, min=-reach, max=reach).astype(held_as)


def setup_inputs(seed: int = 0, part: int = 0) -> dict:
    streams_of = jax.random.split(jax.random.key(seed), 7)
    part_keys = jax.random.split(jax.random.fold_in(streams_of[6], part), 7)
    tokens = draw_tokens(jax.random.fold_in(jax.random.fold_in(streams_of[6], part), 71), part)
    tangent = centred(part_keys[1], (TOKENS, D), 1.0, 6.0, ((0, 16), (1, 8)))
    w_query = centred(streams_of[2], (D, D), D ** -0.5, 0.109375, ((1, 8),))
    w_key = centred(streams_of[3], (D, D), D ** -0.5, 0.109375, ((1, 8),))
    w_value = centred(streams_of[4], (D, D), D ** -0.5, 0.109375, ((1, 8),))
    w_output = centred(streams_of[5], (D, D), (D // 16) ** -0.5, 0.4375, ((0, 8),))
    return dict(tokens=tokens, tangent=tangent, w_query=w_query, w_key=w_key, w_value=w_value, w_output=w_output)


def head_block(query_h, qdot_h, key_h, value_h, kdot_h, vdot_h):
    factor = HEAD_DIM ** -0.5
    scores = jnp.dot(query_h, key_h.T, preferred_element_type=jnp.float32) * factor
    s_dot = (jnp.dot(qdot_h, key_h.T, preferred_element_type=jnp.float32)
             + jnp.dot(query_h, kdot_h.T, preferred_element_type=jnp.float32)) * factor
    top = jnp.max(scores, axis=-1, keepdims=True)
    expo = jnp.exp(scores - top)
    total = jnp.sum(expo, axis=-1, keepdims=True)
    tilt = jnp.sum(expo * s_dot, axis=-1, keepdims=True)
    expo_b = expo.astype(jnp.bfloat16)
    weighted = (expo * s_dot).astype(jnp.bfloat16)
    num_v = jnp.dot(expo_b, value_h, preferred_element_type=jnp.float32)
    num_t = (jnp.dot(weighted, value_h, preferred_element_type=jnp.float32)
             + jnp.dot(expo_b, vdot_h, preferred_element_type=jnp.float32))
    attended = num_v / total
    att_dot = (num_t - (tilt / total) * num_v) / total
    return attended.astype(jnp.bfloat16), att_dot.astype(jnp.bfloat16)


def reference(tokens, tangent, w_query, w_key, w_value, w_output):
    def project(source, weight):
        full = jnp.dot(source, weight, preferred_element_type=jnp.float32).astype(jnp.bfloat16)
        return full.reshape(TOKENS, HEADS, HEAD_DIM).transpose(1, 0, 2)

    query = project(tokens, w_query)
    key = project(tokens, w_key)
    value = project(tokens, w_value)
    q_dot = project(tangent, w_query)
    k_dot = project(tangent, w_key)
    v_dot = project(tangent, w_value)
    block = math.gcd(TOKENS, 512)
    blocks = TOKENS // block

    def one_head(items):
        query_h, qdot_h, key_h, value_h, kdot_h, vdot_h = items

        def one_block(pair):
            return head_block(pair[0], pair[1], key_h, value_h, kdot_h, vdot_h)

        attended, att_dot = lax.map(one_block, (query_h.reshape(blocks, block, HEAD_DIM),
                                                qdot_h.reshape(blocks, block, HEAD_DIM)))
        return attended.reshape(TOKENS, HEAD_DIM), att_dot.reshape(TOKENS, HEAD_DIM)

    attended, att_dot = lax.map(one_head, (query, q_dot, key, value, k_dot, v_dot))
    attended = attended.transpose(1, 0, 2).reshape(TOKENS, D)
    att_dot = att_dot.transpose(1, 0, 2).reshape(TOKENS, D)
    layer_out = jnp.dot(attended, w_output, preferred_element_type=jnp.float32).astype(jnp.bfloat16)
    layer_tangent = jnp.dot(att_dot, w_output, preferred_element_type=jnp.float32).astype(jnp.bfloat16)
    return layer_out, layer_tangent
```

```python
import jax
import jax.numpy as jnp
from jax import lax
from jax.experimental import pallas as pl
from jax.experimental.pallas import tpu as pltpu
from jax.sharding import PartitionSpec as P

MESH = pl.DeviceIdType.MESH
HD = 128
HEADS_HERE = 3
ROWS = 256
COLS = 384
D = 3072
CTX = 16
TP = 8
LANES_KV = 2 * HD
FACTOR = HD ** (-0.5)
LOG2E = 1.4426950408889634
BF16 = jnp.bfloat16
F32 = jnp.float32

GATHERS = ((0, 0, 64), (0, 64, 64), (0, 128, 64), (0, 192, 64), (1, 0, 128), (1, 128, 128))
N_T = 4
N_ITEMS = N_T + HEADS_HERE


def dot_nt(a, b):
    return lax.dot_general(a, b, (((1,), (1,)), ((), ())), preferred_element_type=F32)


def dot_nn(a, b):
    return jnp.dot(a, b, preferred_element_type=F32)


def kernel(
    tok, tan, wq, wk, wv, wo, out_ref, outd_ref,
    xg, wbuf, kvt, kvd, qcat, wt, at, acc_e, acc_w, stat, total,
    loc_sem, g_send, g_recv, z_send, z_recv, s_recv, a_send, a_recv, p_send, p_recv,
):
    dp, ctx, tp = lax.axis_index("dp"), lax.axis_index("ctx"), lax.axis_index("tp")
    core = lax.rem(ctx, 2)
    x, y = tp // 4, lax.rem(tp, 4)
    y_up, y_down, y_far = lax.rem(y + 1, 4), lax.rem(y + 3, 4), lax.rem(y + 2, 4)
    other = 1 - x
    zp = (dp, lax.rem(ctx + 2, CTX), tp)
    zm = (dp, lax.rem(ctx + 14, CTX), tp)
    sib = (dp, ctx + 1 - 2 * core, tp)

    def plane(xx, yy):
        return (dp, ctx, xx * 4 + yy)

    xn, yp, ym = plane(other, y), plane(x, y_up), plane(x, y_down)
    s_x, s_p, s_m = other * 4 + y, x * 4 + y_up, x * 4 + y_down
    s_xp, s_xm = other * 4 + y_up, other * 4 + y_down
    s_f, s_xf = x * 4 + y_far, other * 4 + y_far
    peers = (xn, yp, ym, plane(other, y_up), plane(other, y_down), plane(x, y_far), plane(other, y_far))

    def cols(slot, width):
        return pl.ds(pl.multiple_of(slot * width, 128), width)

    local = [
        pltpu.make_async_copy(tok, xg.at[0, :, cols(tp, COLS)], loc_sem.at[0]),
        pltpu.make_async_copy(tan, xg.at[1, :, cols(tp, COLS)], loc_sem.at[1]),
    ]
    for h in range(HEADS_HERE):
        for j, w in enumerate((wk, wv)):
            local.append(
                pltpu.make_async_copy(
                    w.at[:, pl.ds(h * HD, HD)],
                    wbuf.at[:, pl.ds(h * LANES_KV + j * HD, HD)],
                    loc_sem.at[2 + 2 * h + j],
                )
            )
    local.append(
        pltpu.make_async_copy(wq, wbuf.at[:, pl.ds(3 * LANES_KV, COLS)], loc_sem.at[8])
    )
    local.append(
        pltpu.make_async_copy(
            wo.at[:, pl.ds(core * 64, 64), cols(tp, COLS)], wt.at[:, tp, core], loc_sem.at[9]
        )
    )
    for c in local:
        c.start()

    barrier = pltpu.get_barrier_semaphore()
    greet = (zp, zm, sib) + peers
    for dev in greet:
        pl.semaphore_signal(barrier, inc=1, device_id=dev, device_id_type=MESH)
    pl.semaphore_wait(barrier, len(greet))

    sent = []

    def send(src, dst, ssem, rsem, dev):
        c = pltpu.make_async_remote_copy(
            src_ref=src, dst_ref=dst, send_sem=ssem, recv_sem=rsem, device_id=dev, device_id_type=MESH
        )
        c.start()
        sent.append(c)

    def arrived(ref, ssem, rsem, dev):
        pltpu.make_async_remote_copy(
            src_ref=ref, dst_ref=ref, send_sem=ssem, recv_sem=rsem, device_id=dev, device_id_type=MESH
        ).wait_recv()

    class Gather:
        def __init__(self, view, ssem, rsem, n):
            self.view, self.ssem, self.rsem, self.n = view, ssem, rsem, n

        def go(self, slot, part, j, dev):
            ref = self.part(slot, part)
            send(ref, ref, self.ssem(j), self.rsem(j), dev)

        def part(self, slot, part):
            half = self.n // 2
            lo, n = ((0, self.n), (0, half), (half, half))[part]
            return self.view(slot, lo, n)

        def got(self, slot, part, j):
            arrived(self.part(slot, part), self.ssem(j), self.rsem(j), xn)

        def start(self):
            self.go(tp, 0, 0, xn)
            self.go(tp, 0, 1, yp)
            self.go(tp, 0, 2, ym)

        def step1(self):
            self.got(s_x, 0, 0)
            self.go(s_x, 0, 3, yp)
            self.go(s_x, 0, 4, ym)
            self.got(s_m, 0, 1)
            self.go(s_m, 1, 5, yp)
            self.got(s_p, 0, 2)
            self.go(s_p, 2, 7, ym)

        def step2(self):
            self.got(s_xm, 0, 3)
            self.go(s_xm, 1, 6, yp)
            self.got(s_xp, 0, 4)
            self.go(s_xp, 2, 8, ym)

        def finish(self):
            self.got(s_f, 1, 5)
            self.got(s_xf, 1, 6)
            self.got(s_f, 2, 7)
            self.got(s_xf, 2, 8)

    def acts(g):
        a, r0, n = GATHERS[g]
        return Gather(
            lambda slot, lo, cnt: xg.at[a, pl.ds(r0 + lo, cnt), cols(slot, COLS)],
            lambda j: g_send.at[g, j], lambda j: g_recv.at[g, j], n,
        )

    def heads_out(h):
        return Gather(
            lambda slot, lo, cnt: at.at[h, pl.ds(lo, cnt), cols(slot, HD)],
            lambda j: a_send.at[h, j], lambda j: a_recv.at[h, j], 2 * ROWS,
        )

    def piece(i, c, part):
        if i < N_T:
            _, r0, n = GATHERS[i]
            if part == 0:
                return kvt.at[c, :, :, pl.ds(r0, n)]
            return kvt.at[c, :, part - 1, pl.ds(r0, n)]
        if part == 0:
            return kvd.at[i - N_T, c]
        return kvd.at[i - N_T, c, part - 1]

    def minus(d):
        return lax.rem(ctx + CTX - 2 * d, CTX)

    def plus(d):
        return lax.rem(ctx + 2 * d, CTX)

    def ring_send(i, c, part, j, dev):
        ref = piece(i, c, part)
        send(ref, ref, z_send.at[i, j], z_recv.at[i, j], dev)

    def sib_send(i, c, j):
        ref = piece(i, c, 0)
        send(ref, ref, z_send.at[i, 8 + j], s_recv.at[i, j], sib)

    def ring_got(i, c, part, j):
        arrived(piece(i, c, part), z_send.at[i, j], z_recv.at[i, j], zp)

    def own(i):
        ring_send(i, ctx, 0, 0, zp)
        ring_send(i, ctx, 0, 4, zm)
        sib_send(i, ctx, 0)

    def hop(i, d):
        if d < 4:
            ring_got(i, minus(d), 0, d - 1)
            ring_send(i, minus(d), 0 if d < 3 else 1, d, zp)
            ring_got(i, plus(d), 0, 4 + d - 1)
            ring_send(i, plus(d), 0 if d < 3 else 2, 4 + d, zm)
            sib_send(i, minus(d), 2 * d - 1)
            sib_send(i, plus(d), 2 * d)
        else:
            ring_got(i, minus(4), 1, 3)
            ring_got(i, plus(4), 2, 7)
            sib_send(i, plus(4), 7)

    def sib_got(i, j):
        d = (j + 1) // 2
        pair = ctx + 1 - 2 * core
        c = lax.rem(pair + CTX - 2 * d, CTX) if j % 2 else lax.rem(pair + 2 * d, CTX)
        arrived(piece(i, c, 0), z_send.at[i, 8 + j], s_recv.at[i, j], sib)

    def keys_values_t(g):
        _, r0, n = GATHERS[g]
        for h in range(HEADS_HERE):
            res = dot_nn(xg[0, pl.ds(r0, n), :], wbuf[:, pl.ds(h * LANES_KV, LANES_KV)]).astype(BF16)
            kvt[ctx, h, 0, pl.ds(r0, n), :] = res[:, :HD]
            kvt[ctx, h, 1, pl.ds(r0, n), :] = res[:, HD:]

    def keys_values_d(h):
        res = dot_nn(xg[1], wbuf[:, pl.ds(h * LANES_KV, LANES_KV)]).astype(BF16)
        kvd[h, ctx, 0] = res[:, :HD]
        kvd[h, ctx, 1] = res[:, HD:]

    def queries(a):
        res = dot_nn(xg[a], wbuf[:, pl.ds(3 * LANES_KV, COLS)]).astype(BF16)
        for h in range(HEADS_HERE):
            qcat[h, :, pl.ds((1 - a) * HD, HD)] = res[:, h * HD : (h + 1) * HD]

    def attend(h, chip, first):
        c0 = chip * 2
        kk = kvt[pl.ds(c0, 2), h, 0].reshape(2 * ROWS, HD)
        vv = kvt[pl.ds(c0, 2), h, 1].reshape(2 * ROWS, HD)
        kd = kvd[h, pl.ds(c0, 2), 0].reshape(2 * ROWS, HD)
        vd = kvd[h, pl.ds(c0, 2), 1].reshape(2 * ROWS, HD)
        kcat = jnp.concatenate([kk, kd], axis=1)
        vcat = jnp.concatenate([vv, vd], axis=1)
        for blk in range(2):
            rows = pl.ds(blk * 128, 128)
            qq = qcat[h, rows, :]
            s = dot_nt(qq[:, HD:], kk)
            sd = dot_nt(qq, kcat)
            top = jnp.max(s, axis=1, keepdims=True)
            if not first:
                old = stat[h, 0, rows, :][:, :1]
                top = jnp.maximum(old, top)
            p = jnp.exp2((s - top) * (FACTOR * LOG2E))
            w = p * sd
            l_new = jnp.sum(p, axis=1, keepdims=True)
            t_new = jnp.sum(w, axis=1, keepdims=True)
            e_new = dot_nn(p.astype(BF16), vcat)
            w_new = dot_nn(w.astype(BF16), vv)
            if not first:
                keep = jnp.exp2((old - top) * (FACTOR * LOG2E))
                l_new += stat[h, 1, rows, :][:, :1] * keep
                t_new += stat[h, 2, rows, :][:, :1] * keep
                e_new += acc_e[h, rows, :] * keep
                w_new += acc_w[h, rows, :] * keep
            stat[h, 0, rows, :] = jnp.broadcast_to(top, (128, HD))
            stat[h, 1, rows, :] = jnp.broadcast_to(l_new, (128, HD))
            stat[h, 2, rows, :] = jnp.broadcast_to(t_new, (128, HD))
            acc_e[h, rows, :] = e_new
            acc_w[h, rows, :] = w_new

    me_chip = ctx // 2

    def stage(h, d):
        i = N_T + h
        if h == 0:
            for t in range(N_T):
                for j in ((0,) if d == 0 else ((2 * d - 1, 2 * d) if d < 4 else (7,))):
                    sib_got(t, j)
        for j in ((0,) if d == 0 else ((2 * d - 1, 2 * d) if d < 4 else (7,))):
            sib_got(i, j)
        if d == 0:
            attend(h, me_chip, True)
        elif d == 4:
            attend(h, lax.rem(me_chip + 4, 8), False)
        else:
            def both(k, carry):
                attend(h, lax.rem(me_chip + 8 - d + 2 * d * k, 8), False)
                return carry
            lax.fori_loop(0, 2, both, 0)

    def close(h):
        l = stat[h, 1]
        num_v = acc_e[h, :, pl.ds(0, HD)]
        att = num_v / l
        num_t = acc_w[h] * FACTOR + acc_e[h, :, pl.ds(HD, HD)]
        dot_part = (num_t - (stat[h, 2] * FACTOR / l) * num_v) / l
        at[h, pl.ds(0, ROWS), cols(tp, HD)] = att.astype(BF16)
        at[h, pl.ds(ROWS, ROWS), cols(tp, HD)] = dot_part.astype(BF16)

    def project(h):
        res = dot_nn(at[h], wt[h].reshape(TP * HD, COLS))
        if h == 0:
            total[...] = res
        elif h == 1:
            total[...] += res
        else:
            res = (total[...] + res).astype(BF16)
            out_ref[...] = res[:ROWS]
            outd_ref[...] = res[ROWS:]

    G = [acts(g) for g in range(len(GATHERS))]
    A = [heads_out(h) for h in range(HEADS_HERE)]

    def make_t(g):
        G[g].finish()
        keys_values_t(g)
        own(g)

    local[0].wait()
    G[0].start()
    G[1].start()
    G[0].step1()
    G[1].step1()
    G[0].step2()
    G[2].start()
    G[1].step2()
    for c in local[2:8]:
        c.wait()
    make_t(0)
    G[2].step1()
    G[3].start()
    make_t(1)
    G[2].step2()
    G[3].step1()
    hop(0, 1)
    make_t(2)
    G[3].step2()
    hop(1, 1)
    local[1].wait()
    G[4].start()
    hop(0, 2)
    make_t(3)
    G[5].start()
    hop(2, 1)
    hop(1, 2)
    hop(0, 3)
    local[8].wait()
    queries(0)
    G[4].step1()
    hop(3, 1)
    hop(2, 2)
    hop(1, 3)
    G[5].step1()
    hop(0, 4)
    hop(3, 2)
    hop(2, 3)
    G[4].step2()
    hop(1, 4)
    G[5].step2()
    G[4].finish()
    G[5].finish()
    keys_values_d(0)
    own(4)
    hop(3, 3)
    local[9].wait()
    slots = (s_x, s_p, s_m, s_xp, s_xm, s_f, s_xf)
    for j, dev in enumerate(peers):
        send(
            wo.at[:, pl.ds(core * 64, 64), cols(slots[j], COLS)], wt.at[:, tp, core],
            p_send.at[j], p_recv.at[j], dev,
        )
    keys_values_d(1)
    own(5)
    hop(2, 4)
    hop(4, 1)
    hop(3, 4)
    queries(1)
    stage(0, 0)
    keys_values_d(2)
    hop(5, 1)
    hop(4, 2)
    own(6)
    stage(0, 1)
    stage(1, 0)
    hop(4, 3)
    hop(5, 2)
    stage(0, 2)
    hop(6, 1)
    hop(4, 4)
    stage(1, 1)
    hop(5, 3)
    stage(0, 3)
    stage(0, 4)
    close(0)
    A[0].start()
    stage(2, 0)
    hop(6, 2)
    back = (s_x, s_m, s_p, s_xm, s_xp, s_f, s_xf)
    for j in range(len(peers)):
        arrived(wt.at[:, back[j], core], p_send.at[j], p_recv.at[j], peers[j])
    send(wt.at[:, :, core], wt.at[:, :, core], p_send.at[7], p_recv.at[7], sib)
    hop(5, 4)
    stage(1, 2)
    stage(2, 1)
    A[0].step1()
    stage(1, 3)
    hop(6, 3)
    stage(1, 4)
    close(1)
    A[1].start()
    A[0].step2()
    stage(2, 2)
    A[1].step1()
    hop(6, 4)
    stage(2, 3)
    A[1].step2()
    stage(2, 4)
    close(2)
    A[2].start()
    arrived(wt.at[:, :, 1 - core], p_send.at[7], p_recv.at[7], sib)
    A[0].finish()
    project(0)
    A[2].step1()
    A[1].finish()
    project(1)
    A[2].step2()
    A[2].finish()
    project(2)
    for c in sent:
        c.wait_send()


def body(tokens, tangent, w_query, w_key, w_value, w_output):
    wo = w_output.reshape(HEADS_HERE, HD, D)
    hbm = pl.BlockSpec(memory_space=pl.ANY)
    vmem = pl.BlockSpec(memory_space=pltpu.VMEM)
    dma = pltpu.SemaphoreType.DMA
    n_g = len(GATHERS)
    layer_out, layer_tangent = pl.pallas_call(
        kernel,
        out_shape=[jax.ShapeDtypeStruct((ROWS, COLS), BF16)] * 2,
        in_specs=[hbm] * 6,
        out_specs=[vmem] * 2,
        scratch_shapes=[
            pltpu.VMEM((2, ROWS, D), BF16),
            pltpu.VMEM((D, 3 * COLS), BF16),
            pltpu.VMEM((CTX, HEADS_HERE, 2, ROWS, HD), BF16),
            pltpu.VMEM((HEADS_HERE, CTX, 2, ROWS, HD), BF16),
            pltpu.VMEM((HEADS_HERE, ROWS, 2 * HD), BF16),
            pltpu.VMEM((HEADS_HERE, TP, 2, 64, COLS), BF16),
            pltpu.VMEM((HEADS_HERE, 2 * ROWS, TP * HD), BF16),
            pltpu.VMEM((HEADS_HERE, ROWS, 2 * HD), F32),
            pltpu.VMEM((HEADS_HERE, ROWS, HD), F32),
            pltpu.VMEM((HEADS_HERE, 3, ROWS, HD), F32),
            pltpu.VMEM((2 * ROWS, COLS), F32),
            dma((10,)),
            dma((n_g, 9)),
            dma((n_g, 9)),
            dma((N_ITEMS, 16)),
            dma((N_ITEMS, 8)),
            dma((N_ITEMS, 8)),
            dma((HEADS_HERE, 9)),
            dma((HEADS_HERE, 9)),
            dma((8,)),
            dma((8,)),
        ],
        compiler_params=pltpu.CompilerParams(
            collective_id=0, has_side_effects=True, vmem_limit_bytes=56 << 20
        ),
        cost_estimate=pl.CostEstimate(flops=12_000_000_000, bytes_accessed=40_000_000, transcendentals=3_200_000),
    )(tokens, tangent, w_query, w_key, w_value, wo)
    return layer_out, layer_tangent


def solution(mesh):
    placed = (
        P(("dp", "ctx"), "tp"),
        P(("dp", "ctx"), "tp"),
        P(None, "tp"),
        P(None, "tp"),
        P(None, "tp"),
        P("tp", None),
    )
    return jax.shard_map(
        body,
        mesh=mesh,
        in_specs=placed,
        out_specs=(P(("dp", "ctx"), "tp"), P(("dp", "ctx"), "tp")),
        check_vma=False,
    )
```

```python
import jax
import jax.numpy as jnp
from jax import lax
from jax.experimental import pallas as pl
from jax.experimental.pallas import tpu as pltpu
from jax.sharding import PartitionSpec as P

MESH = pl.DeviceIdType.MESH
HD = 128
HEADS_HERE = 3
ROWS = 256
COLS = 384
D = 3072
CTX = 16
TP = 8
LANES_KV = 2 * HD
FACTOR = HD ** (-0.5)
LOG2E = 1.4426950408889634
BF16 = jnp.bfloat16
F32 = jnp.float32

GATHERS = ((0, 0, 32), (0, 32, 32), (0, 64, 64), (0, 128, 64), (0, 192, 64), (1, 0, 128), (1, 128, 128))
DIRECT = (False, False, False, False, False, False, False)
DIRECT_OUT = (True, True, True, False)
N_T = 5
N_ITEMS = N_T + HEADS_HERE


def dot_nt(a, b):
    return lax.dot_general(a, b, (((1,), (1,)), ((), ())), preferred_element_type=F32)


def dot_nn(a, b):
    return jnp.dot(a, b, preferred_element_type=F32)


def kernel(
    tok, tan, wq, wk, wv, wo, out_ref, outd_ref,
    xg, wbuf, kvt, kvd, qcat, wt, at, acc_v, acc_w, stat, total,
    loc_sem, g_send, g_recv, z_send, z_recv, s_recv, a_send, a_recv, p_send, p_recv,
):
    dp, ctx, tp = lax.axis_index("dp"), lax.axis_index("ctx"), lax.axis_index("tp")
    core = lax.rem(ctx, 2)
    x, y = tp // 4, lax.rem(tp, 4)
    y_up, y_down, y_far = lax.rem(y + 1, 4), lax.rem(y + 3, 4), lax.rem(y + 2, 4)
    other = 1 - x
    zp = (dp, lax.rem(ctx + 2, CTX), tp)
    zm = (dp, lax.rem(ctx + 14, CTX), tp)
    sib = (dp, ctx + 1 - 2 * core, tp)

    def plane(xx, yy):
        return (dp, ctx, xx * 4 + yy)

    xn, yp, ym = plane(other, y), plane(x, y_up), plane(x, y_down)
    xyp, xym = plane(other, y_up), plane(other, y_down)
    s_x, s_p, s_m = other * 4 + y, x * 4 + y_up, x * 4 + y_down
    s_xp, s_xm = other * 4 + y_up, other * 4 + y_down
    s_f, s_xf = x * 4 + y_far, other * 4 + y_far
    peers = (xn, yp, ym, xyp, xym, plane(x, y_far), plane(other, y_far))

    slots = (s_x, s_p, s_m, s_xp, s_xm, s_f, s_xf)
    back = (s_x, s_m, s_p, s_xm, s_xp, s_f, s_xf)

    def cols(slot, width):
        return pl.ds(pl.multiple_of(slot * width, 128), width)

    local = [
        pltpu.make_async_copy(tok, xg.at[0, :, cols(tp, COLS)], loc_sem.at[0]),
        pltpu.make_async_copy(tan, xg.at[1, :, cols(tp, COLS)], loc_sem.at[1]),
    ]
    for h in range(HEADS_HERE):
        for j, w in enumerate((wk, wv)):
            local.append(
                pltpu.make_async_copy(
                    w.at[:, pl.ds(h * HD, HD)],
                    wbuf.at[:, pl.ds(h * LANES_KV + j * HD, HD)],
                    loc_sem.at[2 + 2 * h + j],
                )
            )
    local.append(
        pltpu.make_async_copy(wq, wbuf.at[:, pl.ds(3 * LANES_KV, COLS)], loc_sem.at[8])
    )
    local.append(
        pltpu.make_async_copy(
            wo.at[:, pl.ds(core * 64, 64), cols(tp, COLS)], wt.at[:, tp, core], loc_sem.at[9]
        )
    )
    for c in local:
        c.start()

    barrier = pltpu.get_barrier_semaphore()
    greet = (zp, zm, sib) + peers
    for dev in greet:
        pl.semaphore_signal(barrier, inc=1, device_id=dev, device_id_type=MESH)
    pl.semaphore_wait(barrier, len(greet))

    sent = []

    def send(src, dst, ssem, rsem, dev):
        c = pltpu.make_async_remote_copy(
            src_ref=src, dst_ref=dst, send_sem=ssem, recv_sem=rsem, device_id=dev, device_id_type=MESH
        )
        c.start()
        sent.append(c)

    def arrived(ref, ssem, rsem, dev):
        pltpu.make_async_remote_copy(
            src_ref=ref, dst_ref=ref, send_sem=ssem, recv_sem=rsem, device_id=dev, device_id_type=MESH
        ).wait_recv()

    class Gather:
        def __init__(self, view, ssem, rsem, n, direct):
            self.view, self.ssem, self.rsem, self.n, self.direct = view, ssem, rsem, n, direct

        def part(self, slot, part):
            half = self.n // 2
            lo, n = ((0, self.n), (0, half), (half, half))[part]
            return self.view(slot, lo, n)

        def go(self, slot, part, j, dev):
            ref = self.part(slot, part)
            send(ref, ref, self.ssem(j), self.rsem(j), dev)

        def got(self, slot, part, j):
            arrived(self.part(slot, part), self.ssem(j), self.rsem(j), xn)

        def start(self):
            for j, dev in enumerate(peers if self.direct else peers[:5]):
                self.go(tp, 0, j, dev)

        def fwd(self, k):
            self.got(back[1 + k], 0, 1 + k)
            self.go(back[1 + k], 1 + k % 2, 5 + k, (yp, ym)[k % 2])

        def finish(self):
            if self.direct:
                for j in range(len(peers)):
                    self.got(back[j], 0, j)
            else:
                self.got(s_x, 0, 0)
                for k, slot in enumerate((s_f, s_f, s_xf, s_xf)):
                    self.got(slot, 1 + k % 2, 5 + k)

    def acts(g):
        a, r0, n = GATHERS[g]
        return Gather(
            lambda slot, lo, cnt: xg.at[a, pl.ds(r0 + lo, cnt), cols(slot, COLS)],
            lambda j: g_send.at[g, j], lambda j: g_recv.at[g, j], n, DIRECT[g],
        )

    def heads_out(h):
        if h < HEADS_HERE:
            view = lambda slot, lo, cnt: at.at[h, pl.ds(ROWS + lo, cnt), cols(slot, HD)]
        else:
            view = lambda slot, lo, cnt: at.at[:, pl.ds(lo, cnt), cols(slot, HD)]
        return Gather(view, lambda j: a_send.at[h, j], lambda j: a_recv.at[h, j], ROWS, DIRECT_OUT[h])

    def piece(i, c, part):
        if i < N_T:
            _, r0, n = GATHERS[i]
            if part == 0:
                return kvt.at[c, :, :, pl.ds(r0, n)]
            return kvt.at[c, :, part - 1, pl.ds(r0, n)]
        if part == 0:
            return kvd.at[i - N_T, c]
        return kvd.at[i - N_T, c, part - 1]

    def minus(d):
        return lax.rem(ctx + CTX - 2 * d, CTX)

    def plus(d):
        return lax.rem(ctx + 2 * d, CTX)

    def ring_send(i, c, part, j, dev):
        ref = piece(i, c, part)
        send(ref, ref, z_send.at[i, j], z_recv.at[i, j], dev)

    def sib_send(i, c, j):
        ref = piece(i, c, 0)
        send(ref, ref, z_send.at[i, 8 + j], s_recv.at[i, j], sib)

    def ring_got(i, c, part, j):
        arrived(piece(i, c, part), z_send.at[i, j], z_recv.at[i, j], zp)

    def own(i):
        ring_send(i, ctx, 0, 0, zp)
        ring_send(i, ctx, 0, 4, zm)
        sib_send(i, ctx, 0)

    def hop(i, d):
        if d < 4:
            ring_got(i, minus(d), 0, d - 1)
            ring_send(i, minus(d), 0 if d < 3 else 1, d, zp)
            ring_got(i, plus(d), 0, 4 + d - 1)
            ring_send(i, plus(d), 0 if d < 3 else 2, 4 + d, zm)
            sib_send(i, minus(d), 2 * d - 1)
            sib_send(i, plus(d), 2 * d)
        else:
            ring_got(i, minus(4), 1, 3)
            ring_got(i, plus(4), 2, 7)
            sib_send(i, plus(4), 7)

    def sib_got(i, j):
        d = (j + 1) // 2
        pair = ctx + 1 - 2 * core
        c = lax.rem(pair + CTX - 2 * d, CTX) if j % 2 else lax.rem(pair + 2 * d, CTX)
        arrived(piece(i, c, 0), z_send.at[i, 8 + j], s_recv.at[i, j], sib)

    def keys_values_t(g):
        _, r0, n = GATHERS[g]
        for h in range(HEADS_HERE):
            res = dot_nn(xg[0, pl.ds(r0, n), :], wbuf[:, pl.ds(h * LANES_KV, LANES_KV)]).astype(BF16)
            kvt[ctx, h, 0, pl.ds(r0, n), :] = res[:, :HD]
            kvt[ctx, h, 1, pl.ds(r0, n), :] = res[:, HD:]

    def keys_values_d(h):
        res = dot_nn(xg[1], wbuf[:, pl.ds(h * LANES_KV, LANES_KV)]).astype(BF16)
        kvd[h, ctx, 0] = res[:, :HD]
        kvd[h, ctx, 1] = res[:, HD:]

    def queries(a):
        res = dot_nn(xg[a], wbuf[:, pl.ds(3 * LANES_KV, COLS)]).astype(BF16)
        for h in range(HEADS_HERE):
            qcat[h, :, pl.ds((1 - a) * HD, HD)] = res[:, h * HD : (h + 1) * HD]

    def attend(h, chip, first):
        c0 = chip * 2
        kk = kvt[pl.ds(c0, 2), h, 0].reshape(2 * ROWS, HD)
        vv = kvt[pl.ds(c0, 2), h, 1].reshape(2 * ROWS, HD)
        for blk in range(2):
            rows = pl.ds(blk * 128, 128)
            s = dot_nt(qcat[h, rows, pl.ds(HD, HD)], kk)
            top = jnp.max(s, axis=1, keepdims=True)
            if not first:
                old = stat[h, 0, rows, :][:, :1]
                top = jnp.maximum(old, top)
            p = jnp.exp2((s - top) * (FACTOR * LOG2E))
            l_new = jnp.sum(p, axis=1, keepdims=True)
            v_new = dot_nn(p.astype(BF16), vv)
            if not first:
                keep = jnp.exp2((old - top) * (FACTOR * LOG2E))
                l_new += stat[h, 1, rows, :][:, :1] * keep
                v_new += acc_v[h, rows, :] * keep
            stat[h, 0, rows, :] = jnp.broadcast_to(top, (128, HD))
            stat[h, 1, rows, :] = jnp.broadcast_to(l_new, (128, HD))
            acc_v[h, rows, :] = v_new

    def attend_dot(h, chip, first):
        c0 = chip * 2
        kk = kvt[pl.ds(c0, 2), h, 0].reshape(2 * ROWS, HD)
        vv = kvt[pl.ds(c0, 2), h, 1].reshape(2 * ROWS, HD)
        kd = kvd[h, pl.ds(c0, 2), 0].reshape(2 * ROWS, HD)
        vd = kvd[h, pl.ds(c0, 2), 1].reshape(2 * ROWS, HD)
        kcat = jnp.concatenate([kk, kd], axis=1)
        for blk in range(2):
            rows = pl.ds(blk * 128, 128)
            qq = qcat[h, rows, :]
            s = dot_nt(qq[:, HD:], kk)
            sd = dot_nt(qq, kcat)
            p = jnp.exp2((s - stat[h, 0, rows, :][:, :1]) * (FACTOR * LOG2E))
            w = p * sd
            t_new = jnp.sum(w, axis=1, keepdims=True)
            w_new = dot_nn(w.astype(BF16), vv) * FACTOR + dot_nn(p.astype(BF16), vd)
            if not first:
                t_new += stat[h, 2, rows, :][:, :1]
                w_new += acc_w[h, rows, :]
            stat[h, 2, rows, :] = jnp.broadcast_to(t_new, (128, HD))
            acc_w[h, rows, :] = w_new

    me_chip = ctx // 2

    def arrivals(d):
        return (0,) if d == 0 else ((2 * d - 1, 2 * d) if d < 4 else (7,))

    def over(attending, h, d):
        if d == 0:
            attending(h, me_chip, True)
        elif d == 4:
            attending(h, lax.rem(me_chip + 4, 8), False)
        else:
            def both(k, carry):
                attending(h, lax.rem(me_chip + 8 - d + 2 * d * k, 8), False)
                return carry
            lax.fori_loop(0, 2, both, 0)

    def t_got(d):
        for j in arrivals(d):
            for t in range(N_T):
                sib_got(t, j)

    def d_got(h, d):
        for j in arrivals(d):
            sib_got(N_T + h, j)

    def stage(h, d):
        over(attend, h, d)

    def stage_dot(h, d):
        over(attend_dot, h, d)

    def close():
        for h in range(HEADS_HERE):
            at[h, pl.ds(0, ROWS), cols(tp, HD)] = (acc_v[h] / stat[h, 1]).astype(BF16)

    def close_dot(h):
        l = stat[h, 1]
        res = (acc_w[h] - (stat[h, 2] * FACTOR / l) * acc_v[h]) / l
        at[h, pl.ds(ROWS, ROWS), cols(tp, HD)] = res.astype(BF16)

    def project():
        res = jnp.zeros((ROWS, COLS), F32)
        for h in range(HEADS_HERE):
            res += dot_nn(at[h, pl.ds(0, ROWS), :], wt[h].reshape(TP * HD, COLS))
        out_ref[...] = res.astype(BF16)

    def project_dot(h):
        res = dot_nn(at[h, pl.ds(ROWS, ROWS), :], wt[h].reshape(TP * HD, COLS))
        if h > 0:
            res += total[...]
        if h < HEADS_HERE - 1:
            total[...] = res
        else:
            outd_ref[...] = res.astype(BF16)

    def weights_send(j):
        send(
            wo.at[:, pl.ds(core * 64, 64), cols(slots[j], COLS)], wt.at[:, tp, core],
            p_send.at[j], p_recv.at[j], peers[j],
        )

    def weights_share():
        for j in range(len(peers)):
            arrived(wt.at[:, back[j], core], p_send.at[j], p_recv.at[j], peers[j])
        local[9].wait()
        send(wt.at[:, :, core], wt.at[:, :, core], p_send.at[7], p_recv.at[7], sib)

    def weights_got():
        arrived(wt.at[:, :, 1 - core], p_send.at[7], p_recv.at[7], sib)

    G = [acts(g) for g in range(len(GATHERS))]
    A = [heads_out(h) for h in range(HEADS_HERE + 1)]

    def make_t(g):
        G[g].finish()
        keys_values_t(g)

    def kvw_wait():
        for c in local[2:8]:
            c.wait()

    def d_gathered():
        for g in range(N_T, len(GATHERS)):
            G[g].finish()

    local[0].wait()
    G[0].start()
    G[1].start()
    G[2].start()
    G[0].fwd(0)
    G[0].fwd(1)
    kvw_wait()
    G[1].fwd(0)
    G[1].fwd(1)
    G[0].fwd(2)
    G[3].start()
    G[0].fwd(3)
    G[2].fwd(0)
    G[2].fwd(1)
    G[1].fwd(2)
    G[1].fwd(3)
    G[4].start()
    G[3].fwd(1)
    G[2].fwd(2)
    G[3].fwd(0)
    G[2].fwd(3)
    make_t(0)
    own(0)
    make_t(1)
    G[4].fwd(0)
    G[3].fwd(2)
    G[4].fwd(1)
    own(1)
    local[1].wait()
    G[5].start()
    G[3].fwd(3)
    hop(0, 1)
    make_t(2)
    own(2)
    G[4].fwd(2)
    hop(1, 1)
    G[4].fwd(3)
    hop(0, 2)
    G[5].fwd(1)
    G[5].fwd(0)
    hop(2, 1)
    G[6].start()
    make_t(3)
    hop(1, 2)
    G[5].fwd(2)
    own(3)
    make_t(4)
    hop(0, 3)
    local[8].wait()
    queries(0)
    G[5].fwd(3)
    own(4)
    hop(2, 2)
    G[6].fwd(0)
    G[6].fwd(1)
    hop(1, 3)
    t_got(0)
    stage(0, 0)
    stage(1, 0)
    weights_send(0)
    stage(2, 0)
    hop(3, 1)
    G[6].fwd(2)
    hop(0, 4)
    weights_send(1)
    G[6].fwd(3)
    hop(4, 1)
    t_got(1)
    stage(0, 1)
    hop(1, 4)
    hop(2, 3)
    d_gathered()
    keys_values_d(0)
    keys_values_d(1)
    hop(3, 2)
    keys_values_d(2)
    queries(1)
    weights_send(2)
    stage(1, 1)
    hop(4, 2)
    hop(2, 4)
    stage(2, 1)
    weights_send(3)
    own(5)
    t_got(2)
    stage(0, 2)
    hop(3, 3)
    stage(1, 2)
    hop(4, 3)
    d_got(0, 0)
    weights_send(4)
    stage(2, 2)
    t_got(3)
    stage(0, 3)
    hop(5, 1)
    weights_send(5)
    stage(1, 3)
    hop(3, 4)
    stage(2, 3)
    hop(4, 4)
    own(6)
    d_got(0, 1)
    weights_send(6)
    t_got(4)
    stage(0, 4)
    hop(5, 2)
    d_got(1, 0)
    stage(1, 4)
    stage(2, 4)
    close()
    A[3].start()
    d_got(0, 2)
    stage_dot(0, 0)
    hop(6, 1)
    stage_dot(0, 1)
    stage_dot(0, 2)
    hop(5, 3)
    d_got(1, 1)
    stage_dot(1, 0)
    own(7)
    stage_dot(1, 1)
    A[3].fwd(0)
    A[3].fwd(1)
    hop(6, 2)
    d_got(2, 0)
    d_got(0, 3)
    stage_dot(0, 3)
    hop(5, 4)
    stage_dot(2, 0)
    d_got(1, 2)
    stage_dot(1, 2)
    A[3].fwd(2)
    hop(7, 1)
    d_got(0, 4)
    stage_dot(0, 4)
    close_dot(0)
    A[0].start()
    weights_share()
    hop(6, 3)
    d_got(2, 1)
    stage_dot(2, 1)
    A[3].fwd(3)
    hop(7, 2)
    weights_got()
    d_got(1, 3)
    stage_dot(1, 3)
    hop(6, 4)
    d_got(2, 2)
    stage_dot(2, 2)
    d_got(1, 4)
    stage_dot(1, 4)
    hop(7, 3)
    close_dot(1)
    A[1].start()
    A[0].finish()
    project_dot(0)
    A[3].finish()
    project()
    d_got(2, 3)
    stage_dot(2, 3)
    hop(7, 4)
    d_got(2, 4)
    stage_dot(2, 4)
    close_dot(2)
    A[2].start()
    A[1].finish()
    project_dot(1)
    A[2].finish()
    project_dot(2)
    for c in sent:
        c.wait_send()


def hand_on(a_ref, b_ref, c_ref, d_ref):
    c_ref[...] = a_ref[...]
    d_ref[...] = b_ref[...]


def body(tokens, tangent, w_query, w_key, w_value, w_output):
    wo = w_output.reshape(HEADS_HERE, HD, D)
    hbm = pl.BlockSpec(memory_space=pl.ANY)
    vmem = pl.BlockSpec(memory_space=pltpu.VMEM)
    dma = pltpu.SemaphoreType.DMA
    n_g = len(GATHERS)
    layer_out, layer_tangent = pl.pallas_call(
        kernel,
        out_shape=[jax.ShapeDtypeStruct((ROWS, COLS), BF16)] * 2,
        in_specs=[hbm] * 6,
        out_specs=[vmem] * 2,
        scratch_shapes=[
            pltpu.VMEM((2, ROWS, D), BF16),
            pltpu.VMEM((D, 3 * COLS), BF16),
            pltpu.VMEM((CTX, HEADS_HERE, 2, ROWS, HD), BF16),
            pltpu.VMEM((HEADS_HERE, CTX, 2, ROWS, HD), BF16),
            pltpu.VMEM((HEADS_HERE, ROWS, 2 * HD), BF16),
            pltpu.VMEM((HEADS_HERE, TP, 2, 64, COLS), BF16),
            pltpu.VMEM((HEADS_HERE, 2 * ROWS, TP * HD), BF16),
            pltpu.VMEM((HEADS_HERE, ROWS, HD), F32),
            pltpu.VMEM((HEADS_HERE, ROWS, HD), F32),
            pltpu.VMEM((HEADS_HERE, 3, ROWS, HD), F32),
            pltpu.VMEM((ROWS, COLS), F32),
            dma((10,)),
            dma((n_g, 9)),
            dma((n_g, 9)),
            dma((N_ITEMS, 16)),
            dma((N_ITEMS, 8)),
            dma((N_ITEMS, 8)),
            dma((HEADS_HERE + 1, 9)),
            dma((HEADS_HERE + 1, 9)),
            dma((8,)),
            dma((8,)),
        ],
        compiler_params=pltpu.CompilerParams(
            collective_id=0, has_side_effects=True, vmem_limit_bytes=56 << 20
        ),
        cost_estimate=pl.CostEstimate(flops=12_000_000_000, bytes_accessed=40_000_000, transcendentals=3_200_000),
    )(tokens, tangent, w_query, w_key, w_value, wo)
    return tuple(
        pl.pallas_call(
            hand_on,
            out_shape=[jax.ShapeDtypeStruct((ROWS, COLS), BF16)] * 2,
            in_specs=[vmem] * 2,
            out_specs=[vmem] * 2,
        )(layer_out, layer_tangent)
    )


def solution(mesh):
    placed = (
        P(("dp", "ctx"), "tp"),
        P(("dp", "ctx"), "tp"),
        P(None, "tp"),
        P(None, "tp"),
        P(None, "tp"),
        P("tp", None),
    )
    return jax.shard_map(
        body,
        mesh=mesh,
        in_specs=placed,
        out_specs=(P(("dp", "ctx"), "tp"), P(("dp", "ctx"), "tp")),
        check_vma=False,
    )
```

```python
import jax
import jax.numpy as jnp
from jax import lax
from jax.experimental import pallas as pl
from jax.experimental.pallas import tpu as pltpu
from jax.sharding import PartitionSpec as P

MESH = pl.DeviceIdType.MESH
HD = 128
HEADS_HERE = 3
ROWS = 256
COLS = 384
D = 3072
CTX = 16
TP = 8
LANES_KV = 2 * HD
FACTOR = HD ** (-0.5)
LOG2E = 1.4426950408889634
BF16 = jnp.bfloat16
F32 = jnp.float32

GATHERS = ((0, 0, 32), (0, 32, 32), (0, 64, 32), (0, 96, 32), (0, 128, 64), (0, 192, 64), (1, 0, 64), (1, 64, 64), (1, 128, 64), (1, 192, 64))
DIRECT = (True, True, True, True, True, True, False, False, False, True)
DIRECT_OUT = (False, False, True, True)
N_T = 6
N_ITEMS = N_T + HEADS_HERE


def dot_nt(a, b):
    return lax.dot_general(a, b, (((1,), (1,)), ((), ())), preferred_element_type=F32)


def dot_nn(a, b):
    return jnp.dot(a, b, preferred_element_type=F32)


def kernel(
    tok, tan, wq, wk, wv, wo, out_ref, outd_ref,
    xg, wbuf, kvt, kvd, qcat, wt, at, acc_v, acc_w, stat, total,
    loc_sem, g_send, g_recv, z_send, z_recv, s_recv, a_send, a_recv, p_send, p_recv,
):
    dp, ctx, tp = lax.axis_index("dp"), lax.axis_index("ctx"), lax.axis_index("tp")
    core = lax.rem(ctx, 2)
    x, y = tp // 4, lax.rem(tp, 4)
    y_up, y_down, y_far = lax.rem(y + 1, 4), lax.rem(y + 3, 4), lax.rem(y + 2, 4)
    other = 1 - x
    zp = (dp, lax.rem(ctx + 2, CTX), tp)
    zm = (dp, lax.rem(ctx + 14, CTX), tp)
    sib = (dp, ctx + 1 - 2 * core, tp)

    def plane(xx, yy):
        return (dp, ctx, xx * 4 + yy)

    xn, yp, ym = plane(other, y), plane(x, y_up), plane(x, y_down)
    xyp, xym = plane(other, y_up), plane(other, y_down)
    s_x, s_p, s_m = other * 4 + y, x * 4 + y_up, x * 4 + y_down
    s_xp, s_xm = other * 4 + y_up, other * 4 + y_down
    s_f, s_xf = x * 4 + y_far, other * 4 + y_far
    peers = (xn, yp, ym, xyp, xym, plane(x, y_far), plane(other, y_far))

    slots = (s_x, s_p, s_m, s_xp, s_xm, s_f, s_xf)
    back = (s_x, s_m, s_p, s_xm, s_xp, s_f, s_xf)

    def cols(slot, width):
        return pl.ds(pl.multiple_of(slot * width, 128), width)

    local = [
        pltpu.make_async_copy(tok, xg.at[0, :, cols(tp, COLS)], loc_sem.at[0]),
        pltpu.make_async_copy(tan, xg.at[1, :, cols(tp, COLS)], loc_sem.at[1]),
    ]
    for h in range(HEADS_HERE):
        for j, w in enumerate((wk, wv)):
            local.append(
                pltpu.make_async_copy(
                    w.at[:, pl.ds(h * HD, HD)],
                    wbuf.at[:, pl.ds(h * LANES_KV + j * HD, HD)],
                    loc_sem.at[2 + 2 * h + j],
                )
            )
    local.append(
        pltpu.make_async_copy(wq, wbuf.at[:, pl.ds(3 * LANES_KV, COLS)], loc_sem.at[8])
    )
    local.append(
        pltpu.make_async_copy(
            wo.at[:, pl.ds(core * 64, 64), cols(tp, COLS)], wt.at[:, tp, core], loc_sem.at[9]
        )
    )
    for c in local:
        c.start()

    barrier = pltpu.get_barrier_semaphore()
    greet = (zp, zm, sib) + peers
    for dev in greet:
        pl.semaphore_signal(barrier, inc=1, device_id=dev, device_id_type=MESH)
    pl.semaphore_wait(barrier, len(greet))

    sent = []

    def send(src, dst, ssem, rsem, dev):
        c = pltpu.make_async_remote_copy(
            src_ref=src, dst_ref=dst, send_sem=ssem, recv_sem=rsem, device_id=dev, device_id_type=MESH
        )
        c.start()
        sent.append(c)

    def arrived(ref, ssem, rsem, dev):
        pltpu.make_async_remote_copy(
            src_ref=ref, dst_ref=ref, send_sem=ssem, recv_sem=rsem, device_id=dev, device_id_type=MESH
        ).wait_recv()

    class Gather:
        def __init__(self, view, ssem, rsem, n, direct):
            self.view, self.ssem, self.rsem, self.n, self.direct = view, ssem, rsem, n, direct

        def part(self, slot, part):
            half = self.n // 2
            lo, n = ((0, self.n), (0, half), (half, half))[part]
            return self.view(slot, lo, n)

        def go(self, slot, part, j, dev):
            ref = self.part(slot, part)
            send(ref, ref, self.ssem(j), self.rsem(j), dev)

        def got(self, slot, part, j):
            arrived(self.part(slot, part), self.ssem(j), self.rsem(j), xn)

        def start(self):
            for j, dev in enumerate(peers if self.direct else peers[:5]):
                self.go(tp, 0, j, dev)

        def fwd(self, k):
            self.got(back[1 + k], 0, 1 + k)
            self.go(back[1 + k], 1 + k % 2, 5 + k, (yp, ym)[k % 2])

        def finish(self):
            if self.direct:
                for j in range(len(peers)):
                    self.got(back[j], 0, j)
            else:
                self.got(s_x, 0, 0)
                for k, slot in enumerate((s_f, s_f, s_xf, s_xf)):
                    self.got(slot, 1 + k % 2, 5 + k)

    def acts(g):
        a, r0, n = GATHERS[g]
        return Gather(
            lambda slot, lo, cnt: xg.at[a, pl.ds(r0 + lo, cnt), cols(slot, COLS)],
            lambda j: g_send.at[g, j], lambda j: g_recv.at[g, j], n, DIRECT[g],
        )

    def heads_out(h):
        if h < HEADS_HERE:
            view = lambda slot, lo, cnt: at.at[h, pl.ds(ROWS + lo, cnt), cols(slot, HD)]
        else:
            view = lambda slot, lo, cnt: at.at[:, pl.ds(lo, cnt), cols(slot, HD)]
        return Gather(view, lambda j: a_send.at[h, j], lambda j: a_recv.at[h, j], ROWS, DIRECT_OUT[h])

    def piece(i, c, part):
        if i < N_T:
            _, r0, n = GATHERS[i]
            if part == 0:
                return kvt.at[c, :, :, pl.ds(r0, n)]
            return kvt.at[c, :, part - 1, pl.ds(r0, n)]
        if part == 0:
            return kvd.at[i - N_T, c]
        return kvd.at[i - N_T, c, part - 1]

    def minus(d):
        return lax.rem(ctx + CTX - 2 * d, CTX)

    def plus(d):
        return lax.rem(ctx + 2 * d, CTX)

    def ring_send(i, c, part, j, dev):
        ref = piece(i, c, part)
        send(ref, ref, z_send.at[i, j], z_recv.at[i, j], dev)

    def sib_send(i, c, j):
        ref = piece(i, c, 0)
        send(ref, ref, z_send.at[i, 8 + j], s_recv.at[i, j], sib)

    def ring_got(i, c, part, j):
        arrived(piece(i, c, part), z_send.at[i, j], z_recv.at[i, j], zp)

    def own(i):
        ring_send(i, ctx, 0, 0, zp)
        ring_send(i, ctx, 0, 4, zm)
        sib_send(i, ctx, 0)

    def hop(i, d):
        if d < 4:
            ring_got(i, minus(d), 0, d - 1)
            ring_send(i, minus(d), 0 if d < 3 else 1, d, zp)
            ring_got(i, plus(d), 0, 4 + d - 1)
            ring_send(i, plus(d), 0 if d < 3 else 2, 4 + d, zm)
            sib_send(i, minus(d), 2 * d - 1)
            sib_send(i, plus(d), 2 * d)
        else:
            ring_got(i, minus(4), 1, 3)
            ring_got(i, plus(4), 2, 7)
            sib_send(i, plus(4), 7)

    def sib_got(i, j):
        d = (j + 1) // 2
        pair = ctx + 1 - 2 * core
        c = lax.rem(pair + CTX - 2 * d, CTX) if j % 2 else lax.rem(pair + 2 * d, CTX)
        arrived(piece(i, c, 0), z_send.at[i, 8 + j], s_recv.at[i, j], sib)

    def keys_values_t(g):
        _, r0, n = GATHERS[g]
        for h in range(HEADS_HERE):
            res = dot_nn(xg[0, pl.ds(r0, n), :], wbuf[:, pl.ds(h * LANES_KV, LANES_KV)]).astype(BF16)
            kvt[ctx, h, 0, pl.ds(r0, n), :] = res[:, :HD]
            kvt[ctx, h, 1, pl.ds(r0, n), :] = res[:, HD:]

    def keys_values_d(h):
        res = dot_nn(xg[1], wbuf[:, pl.ds(h * LANES_KV, LANES_KV)]).astype(BF16)
        kvd[h, ctx, 0] = res[:, :HD]
        kvd[h, ctx, 1] = res[:, HD:]

    def queries(a):
        res = dot_nn(xg[a], wbuf[:, pl.ds(3 * LANES_KV, COLS)]).astype(BF16)
        for h in range(HEADS_HERE):
            qcat[h, :, pl.ds((1 - a) * HD, HD)] = res[:, h * HD : (h + 1) * HD]

    ones = jnp.ones((2 * ROWS, HD), BF16)

    def wide(stat_rows):
        return jnp.concatenate([stat_rows] * (2 * ROWS // HD), axis=1)

    def attend(h, chip, first):
        c0 = chip * 2
        kk = kvt[pl.ds(c0, 2), h, 0].reshape(2 * ROWS, HD)
        vv = kvt[pl.ds(c0, 2), h, 1].reshape(2 * ROWS, HD)
        vcat = jnp.concatenate([vv, ones], axis=1)
        for blk in range(2):
            rows = pl.ds(blk * 128, 128)
            s = dot_nt(qcat[h, rows, pl.ds(HD, HD)], kk)
            top = jnp.broadcast_to(jnp.max(s, axis=1, keepdims=True), (128, HD))
            if not first:
                old = stat[h, 0, rows, :]
                top = jnp.maximum(old, top)
                keep = jnp.exp2((old - top) * (FACTOR * LOG2E))
            p = jnp.exp2((s - wide(top)) * (FACTOR * LOG2E)).astype(BF16)
            res = dot_nn(p, vcat)
            v_new, l_new = res[:, :HD], res[:, HD:]
            if not first:
                l_new += stat[h, 1, rows, :] * keep
                v_new += acc_v[h, rows, :] * keep
            stat[h, 0, rows, :] = top
            stat[h, 1, rows, :] = l_new
            acc_v[h, rows, :] = v_new

    def attend_dot(h, chip, first):
        c0 = chip * 2
        kk = kvt[pl.ds(c0, 2), h, 0].reshape(2 * ROWS, HD)
        vv = kvt[pl.ds(c0, 2), h, 1].reshape(2 * ROWS, HD)
        kd = kvd[h, pl.ds(c0, 2), 0].reshape(2 * ROWS, HD)
        vd = kvd[h, pl.ds(c0, 2), 1].reshape(2 * ROWS, HD)
        kcat = jnp.concatenate([kk, kd], axis=1)
        vcat = jnp.concatenate([vv, ones], axis=1)
        qq = qcat[h]
        s = dot_nt(qq[:, HD:], kk)
        sd = dot_nt(qq, kcat)
        p = jnp.exp2((s - wide(stat[h, 0])) * (FACTOR * LOG2E))
        res = dot_nn((p * sd).astype(BF16), vcat)
        w_new = res[:, :HD] * FACTOR + dot_nn(p.astype(BF16), vd)
        t_new = res[:, HD:]
        if not first:
            t_new += stat[h, 2]
            w_new += acc_w[h]
        stat[h, 2] = t_new
        acc_w[h] = w_new

    me_chip = ctx // 2

    def arrivals(d):
        return (0,) if d == 0 else ((2 * d - 1, 2 * d) if d < 4 else (7,))

    def chips(d):
        if d == 0:
            return (me_chip,)
        if d == 4:
            return (lax.rem(me_chip + 4, 8),)
        return (lax.rem(me_chip + 8 - d, 8), lax.rem(me_chip + d, 8))

    def t_got(d):
        for j in arrivals(d):
            for t in range(N_T):
                sib_got(t, j)

    def d_got(h, d):
        for j in arrivals(d):
            sib_got(N_T + h, j)

    def stage(d):
        for chip in chips(d):
            for h in range(HEADS_HERE):
                attend(h, chip, d == 0)

    def stage_dot(h, d):
        for chip in chips(d):
            attend_dot(h, chip, d == 0)

    def close():
        for h in range(HEADS_HERE):
            at[h, pl.ds(0, ROWS), cols(tp, HD)] = (acc_v[h] / stat[h, 1]).astype(BF16)

    def close_dot(h):
        l = stat[h, 1]
        res = (acc_w[h] - (stat[h, 2] * FACTOR / l) * acc_v[h]) / l
        at[h, pl.ds(ROWS, ROWS), cols(tp, HD)] = res.astype(BF16)

    def project():
        res = jnp.zeros((ROWS, COLS), F32)
        for h in range(HEADS_HERE):
            res += dot_nn(at[h, pl.ds(0, ROWS), :], wt[h].reshape(TP * HD, COLS))
        out_ref[...] = res.astype(BF16)

    def project_dot(h):
        res = dot_nn(at[h, pl.ds(ROWS, ROWS), :], wt[h].reshape(TP * HD, COLS))
        if h > 0:
            res += total[...]
        if h < HEADS_HERE - 1:
            total[...] = res
        else:
            outd_ref[...] = res.astype(BF16)

    def weights_send(j):
        send(
            wo.at[:, pl.ds(core * 64, 64), cols(slots[j], COLS)], wt.at[:, tp, core],
            p_send.at[j], p_recv.at[j], peers[j],
        )

    def weights_share():
        for j in range(len(peers)):
            arrived(wt.at[:, back[j], core], p_send.at[j], p_recv.at[j], peers[j])
        local[9].wait()
        send(wt.at[:, :, core], wt.at[:, :, core], p_send.at[7], p_recv.at[7], sib)

    def weights_got():
        arrived(wt.at[:, :, 1 - core], p_send.at[7], p_recv.at[7], sib)

    G = [acts(g) for g in range(len(GATHERS))]
    A = [heads_out(h) for h in range(HEADS_HERE + 1)]

    def make_t(g):
        G[g].finish()
        keys_values_t(g)

    def kvw_wait():
        for c in local[2:8]:
            c.wait()

    def d_gathered():
        for g in range(N_T, len(GATHERS)):
            G[g].finish()

    local[0].wait()
    G[0].start()
    G[1].start()
    G[2].start()
    G[3].start()
    G[4].start()
    kvw_wait()
    make_t(0)
    own(0)
    G[5].start()
    make_t(1)
    own(1)
    hop(0, 1)
    make_t(2)
    own(2)
    local[1].wait()
    G[6].start()
    hop(1, 1)
    make_t(3)
    own(3)
    hop(0, 2)
    hop(2, 1)
    G[7].start()
    hop(1, 2)
    hop(3, 1)
    make_t(4)
    own(4)
    hop(0, 3)
    G[8].start()
    hop(2, 2)
    hop(1, 3)
    G[6].fwd(0)
    hop(3, 2)
    G[6].fwd(1)
    make_t(5)
    local[8].wait()
    queries(0)
    G[6].fwd(2)
    own(5)
    G[7].fwd(0)
    G[7].fwd(1)
    hop(4, 1)
    G[6].fwd(3)
    hop(0, 4)
    G[9].start()
    hop(2, 3)
    t_got(0)
    stage(0)
    hop(1, 4)
    G[8].fwd(0)
    G[7].fwd(2)
    G[8].fwd(1)
    hop(3, 3)
    G[7].fwd(3)
    hop(5, 1)
    weights_send(0)
    G[8].fwd(2)
    G[8].fwd(3)
    t_got(1)
    stage(1)
    hop(4, 2)
    hop(3, 4)
    hop(2, 4)
    weights_send(1)
    weights_send(2)
    weights_send(3)
    hop(5, 2)
    d_gathered()
    keys_values_d(0)
    own(6)
    keys_values_d(1)
    keys_values_d(2)
    t_got(2)
    hop(4, 3)
    d_got(0, 0)
    weights_send(4)
    stage(2)
    own(7)
    hop(5, 3)
    weights_send(5)
    queries(1)
    hop(6, 1)
    d_got(1, 0)
    t_got(3)
    stage(3)
    hop(4, 4)
    weights_send(6)
    d_got(0, 1)
    hop(7, 1)
    hop(5, 4)
    d_got(1, 1)
    t_got(4)
    stage(4)
    close()
    A[3].start()
    hop(6, 2)
    stage_dot(0, 0)
    stage_dot(0, 1)
    stage_dot(1, 0)
    stage_dot(1, 1)
    own(8)
    hop(7, 2)
    d_got(0, 2)
    stage_dot(0, 2)
    weights_share()
    d_got(2, 0)
    stage_dot(2, 0)
    d_got(1, 2)
    stage_dot(1, 2)
    hop(6, 3)
    weights_got()
    d_got(0, 3)
    stage_dot(0, 3)
    hop(8, 1)
    d_got(2, 1)
    hop(7, 3)
    stage_dot(2, 1)
    hop(6, 4)
    d_got(1, 3)
    stage_dot(1, 3)
    d_got(0, 4)
    stage_dot(0, 4)
    close_dot(0)
    A[0].start()
    hop(8, 2)
    hop(7, 4)
    d_got(2, 2)
    stage_dot(2, 2)
    d_got(1, 4)
    stage_dot(1, 4)
    close_dot(1)
    A[1].start()
    A[3].finish()
    A[0].fwd(0)
    A[0].fwd(1)
    hop(8, 3)
    project()
    A[0].fwd(2)
    d_got(2, 3)
    stage_dot(2, 3)
    A[1].fwd(0)
    A[1].fwd(1)
    A[0].fwd(3)
    hop(8, 4)
    d_got(2, 4)
    stage_dot(2, 4)
    close_dot(2)
    A[2].start()
    A[1].fwd(2)
    A[0].finish()
    project_dot(0)
    A[1].fwd(3)
    A[1].finish()
    project_dot(1)
    A[2].finish()
    project_dot(2)
    for c in sent:
        c.wait_send()


def hand_on(a_ref, b_ref, c_ref, d_ref):
    c_ref[...] = a_ref[...]
    d_ref[...] = b_ref[...]


def body(tokens, tangent, w_query, w_key, w_value, w_output):
    wo = w_output.reshape(HEADS_HERE, HD, D)
    hbm = pl.BlockSpec(memory_space=pl.ANY)
    vmem = pl.BlockSpec(memory_space=pltpu.VMEM)
    dma = pltpu.SemaphoreType.DMA
    n_g = len(GATHERS)
    layer_out, layer_tangent = pl.pallas_call(
        kernel,
        out_shape=[jax.ShapeDtypeStruct((ROWS, COLS), BF16)] * 2,
        in_specs=[hbm] * 6,
        out_specs=[vmem] * 2,
        scratch_shapes=[
            pltpu.VMEM((2, ROWS, D), BF16),
            pltpu.VMEM((D, 3 * COLS), BF16),
            pltpu.VMEM((CTX, HEADS_HERE, 2, ROWS, HD), BF16),
            pltpu.VMEM((HEADS_HERE, CTX, 2, ROWS, HD), BF16),
            pltpu.VMEM((HEADS_HERE, ROWS, 2 * HD), BF16),
            pltpu.VMEM((HEADS_HERE, TP, 2, 64, COLS), BF16),
            pltpu.VMEM((HEADS_HERE, 2 * ROWS, TP * HD), BF16),
            pltpu.VMEM((HEADS_HERE, ROWS, HD), F32),
            pltpu.VMEM((HEADS_HERE, ROWS, HD), F32),
            pltpu.VMEM((HEADS_HERE, 3, ROWS, HD), F32),
            pltpu.VMEM((ROWS, COLS), F32),
            dma((10,)),
            dma((n_g, 9)),
            dma((n_g, 9)),
            dma((N_ITEMS, 16)),
            dma((N_ITEMS, 8)),
            dma((N_ITEMS, 8)),
            dma((HEADS_HERE + 1, 9)),
            dma((HEADS_HERE + 1, 9)),
            dma((8,)),
            dma((8,)),
        ],
        compiler_params=pltpu.CompilerParams(
            collective_id=0, has_side_effects=True, vmem_limit_bytes=56 << 20
        ),
        cost_estimate=pl.CostEstimate(flops=12_000_000_000, bytes_accessed=40_000_000, transcendentals=3_200_000),
    )(tokens, tangent, w_query, w_key, w_value, wo)
    return tuple(
        pl.pallas_call(
            hand_on,
            out_shape=[jax.ShapeDtypeStruct((ROWS, COLS), BF16)] * 2,
            in_specs=[vmem] * 2,
            out_specs=[vmem] * 2,
        )(layer_out, layer_tangent)
    )


def solution(mesh):
    placed = (
        P(("dp", "ctx"), "tp"),
        P(("dp", "ctx"), "tp"),
        P(None, "tp"),
        P(None, "tp"),
        P(None, "tp"),
        P("tp", None),
    )
    return jax.shard_map(
        body,
        mesh=mesh,
        in_specs=placed,
        out_specs=(P(("dp", "ctx"), "tp"), P(("dp", "ctx"), "tp")),
        check_vma=False,
    )
```

```python
import jax
import jax.numpy as jnp
from jax import lax
from jax.experimental import pallas as pl
from jax.experimental.pallas import tpu as pltpu
from jax.sharding import PartitionSpec as P

MESH = pl.DeviceIdType.MESH
HD = 128
HEADS_HERE = 3
ROWS = 256
COLS = 384
D = 3072
CTX = 16
TP = 8
LANES_KV = 2 * HD
FACTOR = HD ** (-0.5)
LOG2E = 1.4426950408889634
BF16 = jnp.bfloat16
F32 = jnp.float32

GATHERS = ((0, 0, 32), (0, 32, 32), (0, 64, 32), (0, 96, 64), (0, 160, 64), (0, 224, 32), (1, 0, 64), (1, 64, 64), (1, 128, 64), (1, 192, 64))
DIRECT = (True, True, True, True, True, True, False, False, False, True)
DIRECT_OUT = (False, False, True, False)
N_T = 6
N_ITEMS = N_T + HEADS_HERE


def dot_nt(a, b):
    return lax.dot_general(a, b, (((1,), (1,)), ((), ())), preferred_element_type=F32)


def dot_nn(a, b):
    return jnp.dot(a, b, preferred_element_type=F32)


def kernel(
    tok, tan, wq, wk, wv, wo, out_ref, outd_ref,
    xg, wbuf, kvt, kvd, qcat, wt, at, acc_v, acc_w, stat, total,
    loc_sem, g_send, g_recv, z_send, z_recv, s_recv, a_send, a_recv, p_send, p_recv,
):
    dp, ctx, tp = lax.axis_index("dp"), lax.axis_index("ctx"), lax.axis_index("tp")
    core = lax.rem(ctx, 2)
    x, y = tp // 4, lax.rem(tp, 4)
    y_up, y_down, y_far = lax.rem(y + 1, 4), lax.rem(y + 3, 4), lax.rem(y + 2, 4)
    other = 1 - x
    zp = (dp, lax.rem(ctx + 2, CTX), tp)
    zm = (dp, lax.rem(ctx + 14, CTX), tp)
    sib = (dp, ctx + 1 - 2 * core, tp)

    def plane(xx, yy):
        return (dp, ctx, xx * 4 + yy)

    xn, yp, ym = plane(other, y), plane(x, y_up), plane(x, y_down)
    xyp, xym = plane(other, y_up), plane(other, y_down)
    s_x, s_p, s_m = other * 4 + y, x * 4 + y_up, x * 4 + y_down
    s_xp, s_xm = other * 4 + y_up, other * 4 + y_down
    s_f, s_xf = x * 4 + y_far, other * 4 + y_far
    peers = (xn, yp, ym, xyp, xym, plane(x, y_far), plane(other, y_far))

    slots = (s_x, s_p, s_m, s_xp, s_xm, s_f, s_xf)
    back = (s_x, s_m, s_p, s_xm, s_xp, s_f, s_xf)

    def cols(slot, width):
        return pl.ds(pl.multiple_of(slot * width, 128), width)

    local = [
        pltpu.make_async_copy(tok, xg.at[0, :, cols(tp, COLS)], loc_sem.at[0]),
        pltpu.make_async_copy(tan, xg.at[1, :, cols(tp, COLS)], loc_sem.at[1]),
    ]
    for h in range(HEADS_HERE):
        for j, w in enumerate((wk, wv)):
            local.append(
                pltpu.make_async_copy(
                    w.at[:, pl.ds(h * HD, HD)],
                    wbuf.at[:, pl.ds(h * LANES_KV + j * HD, HD)],
                    loc_sem.at[2 + 2 * h + j],
                )
            )
    local.append(
        pltpu.make_async_copy(wq, wbuf.at[:, pl.ds(3 * LANES_KV, COLS)], loc_sem.at[8])
    )
    local.append(
        pltpu.make_async_copy(
            wo.at[:, pl.ds(core * 64, 64), cols(tp, COLS)], wt.at[:, tp, core], loc_sem.at[9]
        )
    )
    for c in local:
        c.start()

    barrier = pltpu.get_barrier_semaphore()
    greet = (zp, zm, sib) + peers
    for dev in greet:
        pl.semaphore_signal(barrier, inc=1, device_id=dev, device_id_type=MESH)
    pl.semaphore_wait(barrier, len(greet))

    sent = []

    def send(src, dst, ssem, rsem, dev):
        c = pltpu.make_async_remote_copy(
            src_ref=src, dst_ref=dst, send_sem=ssem, recv_sem=rsem, device_id=dev, device_id_type=MESH
        )
        c.start()
        sent.append(c)

    def arrived(ref, ssem, rsem, dev):
        pltpu.make_async_remote_copy(
            src_ref=ref, dst_ref=ref, send_sem=ssem, recv_sem=rsem, device_id=dev, device_id_type=MESH
        ).wait_recv()

    class Gather:
        def __init__(self, view, ssem, rsem, n, direct):
            self.view, self.ssem, self.rsem, self.n, self.direct = view, ssem, rsem, n, direct

        def part(self, slot, part):
            half = self.n // 2
            lo, n = ((0, self.n), (0, half), (half, half))[part]
            return self.view(slot, lo, n)

        def go(self, slot, part, j, dev):
            ref = self.part(slot, part)
            send(ref, ref, self.ssem(j), self.rsem(j), dev)

        def got(self, slot, part, j):
            arrived(self.part(slot, part), self.ssem(j), self.rsem(j), xn)

        def start(self):
            for j in (6, 5, 3, 4, 0, 1, 2) if self.direct else (3, 4, 1, 2, 0):
                self.go(tp, 0, j, peers[j])

        def fwd(self, k):
            self.got(back[1 + k], 0, 1 + k)
            self.go(back[1 + k], 1 + k % 2, 5 + k, (yp, ym)[k % 2])

        def finish(self):
            if self.direct:
                for j in range(len(peers)):
                    self.got(back[j], 0, j)
            else:
                self.got(s_x, 0, 0)
                for k, slot in enumerate((s_f, s_f, s_xf, s_xf)):
                    self.got(slot, 1 + k % 2, 5 + k)

    def acts(g):
        a, r0, n = GATHERS[g]
        return Gather(
            lambda slot, lo, cnt: xg.at[a, pl.ds(r0 + lo, cnt), cols(slot, COLS)],
            lambda j: g_send.at[g, j], lambda j: g_recv.at[g, j], n, DIRECT[g],
        )

    def heads_out(h):
        if h < HEADS_HERE:
            view = lambda slot, lo, cnt: at.at[h, pl.ds(ROWS + lo, cnt), cols(slot, HD)]
        else:
            view = lambda slot, lo, cnt: at.at[:, pl.ds(lo, cnt), cols(slot, HD)]
        return Gather(view, lambda j: a_send.at[h, j], lambda j: a_recv.at[h, j], ROWS, DIRECT_OUT[h])

    def piece(i, c, part):
        if i < N_T:
            _, r0, n = GATHERS[i]
            if part == 0:
                return kvt.at[c, :, :, pl.ds(r0, n)]
            return kvt.at[c, :, part - 1, pl.ds(r0, n)]
        if part == 0:
            return kvd.at[i - N_T, c]
        return kvd.at[i - N_T, c, part - 1]

    def minus(d):
        return lax.rem(ctx + CTX - 2 * d, CTX)

    def plus(d):
        return lax.rem(ctx + 2 * d, CTX)

    def ring_send(i, c, part, j, dev):
        ref = piece(i, c, part)
        send(ref, ref, z_send.at[i, j], z_recv.at[i, j], dev)

    def sib_send(i, c, j):
        ref = piece(i, c, 0)
        send(ref, ref, z_send.at[i, 8 + j], s_recv.at[i, j], sib)

    def ring_got(i, c, part, j):
        arrived(piece(i, c, part), z_send.at[i, j], z_recv.at[i, j], zp)

    def own(i):
        ring_send(i, ctx, 0, 0, zp)
        ring_send(i, ctx, 0, 4, zm)
        sib_send(i, ctx, 0)

    def hop(i, d):
        if d < 4:
            ring_got(i, minus(d), 0, d - 1)
            ring_send(i, minus(d), 0 if d < 3 else 1, d, zp)
            ring_got(i, plus(d), 0, 4 + d - 1)
            ring_send(i, plus(d), 0 if d < 3 else 2, 4 + d, zm)
            sib_send(i, minus(d), 2 * d - 1)
            sib_send(i, plus(d), 2 * d)
        else:
            ring_got(i, minus(4), 1, 3)
            ring_got(i, plus(4), 2, 7)
            sib_send(i, plus(4), 7)

    def sib_got(i, j):
        d = (j + 1) // 2
        pair = ctx + 1 - 2 * core
        c = lax.rem(pair + CTX - 2 * d, CTX) if j % 2 else lax.rem(pair + 2 * d, CTX)
        arrived(piece(i, c, 0), z_send.at[i, 8 + j], s_recv.at[i, j], sib)

    def keys_values_t(g):
        _, r0, n = GATHERS[g]
        for h in range(HEADS_HERE):
            res = dot_nn(xg[0, pl.ds(r0, n), :], wbuf[:, pl.ds(h * LANES_KV, LANES_KV)]).astype(BF16)
            kvt[ctx, h, 0, pl.ds(r0, n), :] = res[:, :HD]
            kvt[ctx, h, 1, pl.ds(r0, n), :] = res[:, HD:]

    def keys_values_d(h):
        res = dot_nn(xg[1], wbuf[:, pl.ds(h * LANES_KV, LANES_KV)]).astype(BF16)
        kvd[h, ctx, 0] = res[:, :HD]
        kvd[h, ctx, 1] = res[:, HD:]

    def queries(a):
        res = dot_nn(xg[a], wbuf[:, pl.ds(3 * LANES_KV, COLS)]).astype(BF16)
        for h in range(HEADS_HERE):
            qcat[h, :, pl.ds((1 - a) * HD, HD)] = res[:, h * HD : (h + 1) * HD]

    ones = jnp.ones((2 * ROWS, HD), BF16)

    def wide(stat_rows):
        return jnp.concatenate([stat_rows] * (2 * ROWS // HD), axis=1)

    def attend(h, chip, first):
        c0 = chip * 2
        kk = kvt[pl.ds(c0, 2), h, 0].reshape(2 * ROWS, HD)
        vv = kvt[pl.ds(c0, 2), h, 1].reshape(2 * ROWS, HD)
        vcat = jnp.concatenate([vv, ones], axis=1)
        for blk in range(2):
            rows = pl.ds(blk * 128, 128)
            s = dot_nt(qcat[h, rows, pl.ds(HD, HD)], kk)
            top = jnp.broadcast_to(jnp.max(s, axis=1, keepdims=True), (128, HD))
            if not first:
                old = stat[h, 0, rows, :]
                top = jnp.maximum(old, top)
                keep = jnp.exp2((old - top) * (FACTOR * LOG2E))
            p = jnp.exp2((s - wide(top)) * (FACTOR * LOG2E)).astype(BF16)
            res = dot_nn(p, vcat)
            v_new, l_new = res[:, :HD], res[:, HD:]
            if not first:
                l_new += stat[h, 1, rows, :] * keep
                v_new += acc_v[h, rows, :] * keep
            stat[h, 0, rows, :] = top
            stat[h, 1, rows, :] = l_new
            acc_v[h, rows, :] = v_new

    def attend_dot(h, chip, first):
        c0 = chip * 2
        kk = kvt[pl.ds(c0, 2), h, 0].reshape(2 * ROWS, HD)
        vv = kvt[pl.ds(c0, 2), h, 1].reshape(2 * ROWS, HD)
        kd = kvd[h, pl.ds(c0, 2), 0].reshape(2 * ROWS, HD)
        vd = kvd[h, pl.ds(c0, 2), 1].reshape(2 * ROWS, HD)
        kcat = jnp.concatenate([kk, kd], axis=1)
        vcat = jnp.concatenate([vv, ones], axis=1)
        qq = qcat[h]
        s = dot_nt(qq[:, HD:], kk)
        sd = dot_nt(qq, kcat)
        p = jnp.exp2((s - wide(stat[h, 0])) * (FACTOR * LOG2E))
        res = dot_nn((p * sd).astype(BF16), vcat)
        w_new = res[:, :HD] * FACTOR + dot_nn(p.astype(BF16), vd)
        t_new = res[:, HD:]
        if not first:
            t_new += stat[h, 2]
            w_new += acc_w[h]
        stat[h, 2] = t_new
        acc_w[h] = w_new

    me_chip = ctx // 2

    def arrivals(d):
        return (0,) if d == 0 else ((2 * d - 1, 2 * d) if d < 4 else (7,))

    def chips(d):
        if d == 0:
            return (me_chip,)
        if d == 4:
            return (lax.rem(me_chip + 4, 8),)
        return (lax.rem(me_chip + 8 - d, 8), lax.rem(me_chip + d, 8))

    def t_got(d):
        for j in arrivals(d):
            for t in range(N_T):
                sib_got(t, j)

    def d_got(h, d):
        for j in arrivals(d):
            sib_got(N_T + h, j)

    def stage(d):
        for chip in chips(d):
            for h in range(HEADS_HERE):
                attend(h, chip, d == 0)

    def stage_dot(h, d):
        for chip in chips(d):
            attend_dot(h, chip, d == 0)

    def close():
        for h in range(HEADS_HERE):
            at[h, pl.ds(0, ROWS), cols(tp, HD)] = (acc_v[h] / stat[h, 1]).astype(BF16)

    def close_dot(h):
        l = stat[h, 1]
        res = (acc_w[h] - (stat[h, 2] * FACTOR / l) * acc_v[h]) / l
        at[h, pl.ds(ROWS, ROWS), cols(tp, HD)] = res.astype(BF16)

    def project():
        res = jnp.zeros((ROWS, COLS), F32)
        for h in range(HEADS_HERE):
            res += dot_nn(at[h, pl.ds(0, ROWS), :], wt[h].reshape(TP * HD, COLS))
        out_ref[...] = res.astype(BF16)

    def project_dot(h):
        res = dot_nn(at[h, pl.ds(ROWS, ROWS), :], wt[h].reshape(TP * HD, COLS))
        if h > 0:
            res += total[...]
        if h < HEADS_HERE - 1:
            total[...] = res
        else:
            outd_ref[...] = res.astype(BF16)

    def weights_send(j):
        send(
            wo.at[:, pl.ds(core * 64, 64), cols(slots[j], COLS)], wt.at[:, tp, core],
            p_send.at[j], p_recv.at[j], peers[j],
        )

    def weights_share():
        for j in range(len(peers)):
            arrived(wt.at[:, back[j], core], p_send.at[j], p_recv.at[j], peers[j])
        local[9].wait()
        send(wt.at[:, :, core], wt.at[:, :, core], p_send.at[7], p_recv.at[7], sib)

    def weights_got():
        arrived(wt.at[:, :, 1 - core], p_send.at[7], p_recv.at[7], sib)

    G = [acts(g) for g in range(len(GATHERS))]
    A = [heads_out(h) for h in range(HEADS_HERE + 1)]

    def make_t(g):
        G[g].finish()
        keys_values_t(g)

    def kvw_wait():
        for c in local[2:8]:
            c.wait()

    def d_gathered():
        for g in range(N_T, len(GATHERS)):
            G[g].finish()

    local[0].wait()
    G[0].start()
    G[1].start()
    G[2].start()
    kvw_wait()
    make_t(0)
    own(0)
    G[3].start()
    make_t(1)
    own(1)
    hop(0, 1)
    make_t(2)
    own(2)
    G[4].start()
    hop(1, 1)
    hop(0, 2)
    hop(2, 1)
    make_t(3)
    own(3)
    G[5].start()
    hop(1, 2)
    local[1].wait()
    G[6].start()
    hop(0, 3)
    hop(2, 2)
    G[7].start()
    make_t(4)
    own(4)
    hop(3, 1)
    hop(1, 3)
    make_t(5)
    hop(0, 4)
    own(5)
    G[8].start()
    hop(2, 3)
    G[6].fwd(2)
    local[8].wait()
    queries(0)
    G[6].fwd(0)
    G[6].fwd(1)
    G[6].fwd(3)
    t_got(0)
    stage(0)
    hop(4, 1)
    G[9].start()
    G[7].fwd(0)
    G[7].fwd(1)
    G[7].fwd(2)
    hop(3, 2)
    G[7].fwd(3)
    hop(1, 4)
    G[8].fwd(0)
    G[8].fwd(1)
    hop(5, 1)
    hop(2, 4)
    G[8].fwd(2)
    weights_send(0)
    t_got(1)
    stage(1)
    G[8].fwd(3)
    hop(4, 2)
    weights_send(1)
    weights_send(2)
    weights_send(3)
    hop(3, 3)
    hop(5, 2)
    d_gathered()
    keys_values_d(0)
    own(6)
    keys_values_d(1)
    hop(4, 3)
    keys_values_d(2)
    hop(3, 4)
    d_got(0, 0)
    t_got(2)
    weights_send(4)
    stage(2)
    hop(5, 3)
    weights_send(5)
    queries(1)
    own(7)
    weights_send(6)
    t_got(3)
    stage(3)
    hop(6, 1)
    hop(4, 4)
    d_got(1, 0)
    hop(5, 4)
    d_got(0, 1)
    t_got(4)
    stage(4)
    stage_dot(1, 0)
    hop(7, 1)
    close()
    stage_dot(0, 0)
    stage_dot(0, 1)
    A[3].start()
    d_got(1, 1)
    stage_dot(1, 1)
    hop(6, 2)
    weights_share()
    d_got(0, 2)
    stage_dot(0, 2)
    own(8)
    hop(7, 2)
    hop(6, 3)
    A[3].fwd(2)
    d_got(2, 0)
    stage_dot(2, 0)
    weights_got()
    d_got(1, 2)
    stage_dot(1, 2)
    d_got(0, 3)
    stage_dot(0, 3)
    hop(8, 1)
    A[3].fwd(0)
    A[3].fwd(1)
    A[3].fwd(3)
    d_got(2, 1)
    stage_dot(2, 1)
    hop(7, 3)
    hop(6, 4)
    d_got(1, 3)
    stage_dot(1, 3)
    d_got(0, 4)
    stage_dot(0, 4)
    close_dot(0)
    A[0].start()
    hop(8, 2)
    A[3].finish()
    project()
    hop(7, 4)
    d_got(2, 2)
    stage_dot(2, 2)
    d_got(1, 4)
    stage_dot(1, 4)
    A[0].fwd(2)
    close_dot(1)
    A[1].start()
    A[0].fwd(0)
    A[0].fwd(1)
    hop(8, 3)
    A[0].fwd(3)
    d_got(2, 3)
    stage_dot(2, 3)
    hop(8, 4)
    A[1].fwd(2)
    A[1].fwd(1)
    A[1].fwd(0)
    A[1].fwd(3)
    d_got(2, 4)
    stage_dot(2, 4)
    close_dot(2)
    A[2].start()
    A[0].finish()
    project_dot(0)
    A[1].finish()
    project_dot(1)
    A[2].finish()
    project_dot(2)
    for c in sent:
        c.wait_send()


def hand_on(a_ref, b_ref, c_ref, d_ref):
    c_ref[...] = a_ref[...]
    d_ref[...] = b_ref[...]


def body(tokens, tangent, w_query, w_key, w_value, w_output):
    wo = w_output.reshape(HEADS_HERE, HD, D)
    hbm = pl.BlockSpec(memory_space=pl.ANY)
    vmem = pl.BlockSpec(memory_space=pltpu.VMEM)
    dma = pltpu.SemaphoreType.DMA
    n_g = len(GATHERS)
    layer_out, layer_tangent = pl.pallas_call(
        kernel,
        out_shape=[jax.ShapeDtypeStruct((ROWS, COLS), BF16)] * 2,
        in_specs=[hbm] * 6,
        out_specs=[vmem] * 2,
        scratch_shapes=[
            pltpu.VMEM((2, ROWS, D), BF16),
            pltpu.VMEM((D, 3 * COLS), BF16),
            pltpu.VMEM((CTX, HEADS_HERE, 2, ROWS, HD), BF16),
            pltpu.VMEM((HEADS_HERE, CTX, 2, ROWS, HD), BF16),
            pltpu.VMEM((HEADS_HERE, ROWS, 2 * HD), BF16),
            pltpu.VMEM((HEADS_HERE, TP, 2, 64, COLS), BF16),
            pltpu.VMEM((HEADS_HERE, 2 * ROWS, TP * HD), BF16),
            pltpu.VMEM((HEADS_HERE, ROWS, HD), F32),
            pltpu.VMEM((HEADS_HERE, ROWS, HD), F32),
            pltpu.VMEM((HEADS_HERE, 3, ROWS, HD), F32),
            pltpu.VMEM((ROWS, COLS), F32),
            dma((10,)),
            dma((n_g, 9)),
            dma((n_g, 9)),
            dma((N_ITEMS, 16)),
            dma((N_ITEMS, 8)),
            dma((N_ITEMS, 8)),
            dma((HEADS_HERE + 1, 9)),
            dma((HEADS_HERE + 1, 9)),
            dma((8,)),
            dma((8,)),
        ],
        compiler_params=pltpu.CompilerParams(
            collective_id=0, has_side_effects=True, vmem_limit_bytes=56 << 20
        ),
        cost_estimate=pl.CostEstimate(flops=12_000_000_000, bytes_accessed=40_000_000, transcendentals=3_200_000),
    )(tokens, tangent, w_query, w_key, w_value, wo)
    return tuple(
        pl.pallas_call(
            hand_on,
            out_shape=[jax.ShapeDtypeStruct((ROWS, COLS), BF16)] * 2,
            in_specs=[vmem] * 2,
            out_specs=[vmem] * 2,
        )(layer_out, layer_tangent)
    )


def solution(mesh):
    placed = (
        P(("dp", "ctx"), "tp"),
        P(("dp", "ctx"), "tp"),
        P(None, "tp"),
        P(None, "tp"),
        P(None, "tp"),
        P("tp", None),
    )
    return jax.shard_map(
        body,
        mesh=mesh,
        in_specs=placed,
        out_specs=(P(("dp", "ctx"), "tp"), P(("dp", "ctx"), "tp")),
        check_vma=False,
    )
```

```python
import jax
import jax.numpy as jnp
from jax import lax
from jax.experimental import pallas as pl
from jax.experimental.pallas import tpu as pltpu
from jax.sharding import PartitionSpec as P

MESH = pl.DeviceIdType.MESH
HD = 128
HEADS_HERE = 3
ROWS = 256
COLS = 384
D = 3072
CTX = 16
TP = 8
LANES_KV = 2 * HD
FACTOR = HD ** (-0.5)
LOG2E = 1.4426950408889634
BF16 = jnp.bfloat16
F32 = jnp.float32

GATHERS = ((0, 0, 32), (0, 32, 32), (0, 64, 32), (0, 96, 64), (0, 160, 64), (0, 224, 32), (1, 0, 64), (1, 64, 64), (1, 128, 128))
DIRECT = (True, True, True, False, False, False, False, True, True)
DIRECT_OUT = (False, True, True, False)
N_T = 6
PIECES = ((0, 0, 128), (0, 128, 128), (1, 0, 256), (2, 0, 64), (2, 64, 192))
N_ITEMS = N_T + len(PIECES)


def dot_nt(a, b):
    return lax.dot_general(a, b, (((1,), (1,)), ((), ())), preferred_element_type=F32)


def dot_nn(a, b):
    return jnp.dot(a, b, preferred_element_type=F32)


def kernel(
    tok, tan, wq, wk, wv, wo, out_ref, outd_ref,
    xg, wbuf, kvt, kvd, qcat, wt, at, acc_v, acc_w, stat, total,
    loc_sem, g_send, g_recv, z_send, z_recv, s_recv, a_send, a_recv, p_send, p_recv,
):
    dp, ctx, tp = lax.axis_index("dp"), lax.axis_index("ctx"), lax.axis_index("tp")
    core = lax.rem(ctx, 2)
    x, y = tp // 4, lax.rem(tp, 4)
    y_up, y_down, y_far = lax.rem(y + 1, 4), lax.rem(y + 3, 4), lax.rem(y + 2, 4)
    other = 1 - x
    zp = (dp, lax.rem(ctx + 2, CTX), tp)
    zm = (dp, lax.rem(ctx + 14, CTX), tp)
    sib = (dp, ctx + 1 - 2 * core, tp)

    def plane(xx, yy):
        return (dp, ctx, xx * 4 + yy)

    xn, yp, ym = plane(other, y), plane(x, y_up), plane(x, y_down)
    xyp, xym = plane(other, y_up), plane(other, y_down)
    s_x, s_p, s_m = other * 4 + y, x * 4 + y_up, x * 4 + y_down
    s_xp, s_xm = other * 4 + y_up, other * 4 + y_down
    s_f, s_xf = x * 4 + y_far, other * 4 + y_far
    peers = (xn, yp, ym, xyp, xym, plane(x, y_far), plane(other, y_far))

    slots = (s_x, s_p, s_m, s_xp, s_xm, s_f, s_xf)
    back = (s_x, s_m, s_p, s_xm, s_xp, s_f, s_xf)

    def cols(slot, width):
        return pl.ds(pl.multiple_of(slot * width, 128), width)

    local = [
        pltpu.make_async_copy(tok, xg.at[0, :, cols(tp, COLS)], loc_sem.at[0]),
        pltpu.make_async_copy(tan, xg.at[1, :, cols(tp, COLS)], loc_sem.at[1]),
    ]
    for h in range(HEADS_HERE):
        for j, w in enumerate((wk, wv)):
            local.append(
                pltpu.make_async_copy(
                    w.at[:, pl.ds(h * HD, HD)],
                    wbuf.at[:, pl.ds(h * LANES_KV + j * HD, HD)],
                    loc_sem.at[2 + 2 * h + j],
                )
            )
    local.append(
        pltpu.make_async_copy(wq, wbuf.at[:, pl.ds(3 * LANES_KV, COLS)], loc_sem.at[8])
    )
    local.append(
        pltpu.make_async_copy(
            wo.at[:, pl.ds(core * 64, 64), cols(tp, COLS)], wt.at[:, tp, core], loc_sem.at[9]
        )
    )
    for c in local:
        c.start()

    barrier = pltpu.get_barrier_semaphore()
    greet = (zp, zm, sib) + peers
    for dev in greet:
        pl.semaphore_signal(barrier, inc=1, device_id=dev, device_id_type=MESH)
    pl.semaphore_wait(barrier, len(greet))

    def send(src, dst, ssem, rsem, dev):
        pltpu.make_async_remote_copy(
            src_ref=src, dst_ref=dst, send_sem=ssem, recv_sem=rsem, device_id=dev, device_id_type=MESH
        ).start()

    def left(ref, ssem, rsem):
        pltpu.make_async_remote_copy(
            src_ref=ref, dst_ref=ref, send_sem=ssem, recv_sem=rsem, device_id=xn, device_id_type=MESH
        ).wait_send()

    def arrived(ref, ssem, rsem, dev):
        pltpu.make_async_remote_copy(
            src_ref=ref, dst_ref=ref, send_sem=ssem, recv_sem=rsem, device_id=dev, device_id_type=MESH
        ).wait_recv()

    class Gather:
        def __init__(self, view, blocks, ssem, rsem, n, direct):
            self.view, self.blocks, self.n, self.direct = view, blocks, n, direct
            self.ssem, self.rsem = ssem, rsem

        def part(self, slot, part):
            half = self.n // 2
            lo, n = ((0, self.n), (0, half), (half, half))[part]
            return self.view(slot, lo, n)

        def go(self, slot, part, j, dev):
            ref = self.part(slot, part)
            send(ref, ref, self.ssem(0), self.rsem(j), dev)

        def start(self):
            for j in (6, 5, 3, 4, 0, 1, 2) if self.direct else (3, 4, 1, 2, 0):
                self.go(tp, 0, 0 if self.direct else j, peers[j])

        def fwd(self, k):
            arrived(self.part(back[1 + k], 0), self.ssem(0), self.rsem(1 + k), xn)
            self.go(back[1 + k], 1 + k % 2, 0, (yp, ym)[k % 2])

        def finish(self):
            arrived(self.blocks(7 if self.direct else 3), self.ssem(0), self.rsem(0), xn)

        def done(self):
            left(self.blocks(7), self.ssem(0), self.rsem(0))

    def acts(g):
        a, r0, n = GATHERS[g]
        return Gather(
            lambda slot, lo, cnt: xg.at[a, pl.ds(r0 + lo, cnt), cols(slot, COLS)],
            lambda cnt: xg.at[a, pl.ds(r0, n), pl.ds(0, cnt * COLS)],
            lambda j: g_send.at[g, j], lambda j: g_recv.at[g, j], n, DIRECT[g],
        )

    def heads_out(h):
        if h < HEADS_HERE:
            view = lambda slot, lo, cnt: at.at[h, pl.ds(ROWS + lo, cnt), cols(slot, HD)]
            blocks = lambda cnt: at.at[h, pl.ds(ROWS, ROWS), pl.ds(0, cnt * HD)]
        else:
            view = lambda slot, lo, cnt: at.at[:, pl.ds(lo, cnt), cols(slot, HD)]
            blocks = lambda cnt: at.at[:, pl.ds(0, ROWS), pl.ds(0, cnt * HD)]
        return Gather(view, blocks, lambda j: a_send.at[h, j], lambda j: a_recv.at[h, j], ROWS, DIRECT_OUT[h])

    def piece(i, c, part):
        if i < N_T:
            _, r0, n = GATHERS[i]
            if part == 0:
                return kvt.at[c, :, :, pl.ds(r0, n)]
            return kvt.at[c, :, part - 1, pl.ds(r0, n)]
        h, r0, n = PIECES[i - N_T]
        if part == 0:
            return kvd.at[h, c, :, pl.ds(r0, n)]
        return kvd.at[h, c, part - 1, pl.ds(r0, n)]

    def minus(d):
        return lax.rem(ctx + CTX - 2 * d, CTX)

    def plus(d):
        return lax.rem(ctx + 2 * d, CTX)

    def ring_send(i, c, part, j, dev):
        ref = piece(i, c, part)
        send(ref, ref, z_send.at[i], z_recv.at[i, j], dev)

    def shared(i):
        return 0 if i < N_T else 1 + PIECES[i - N_T][0]

    def sib_send(i, c, j):
        ref = piece(i, c, 0)
        send(ref, ref, z_send.at[i], s_recv.at[shared(i), j], sib)

    def ring_got(i, c, part, j):
        arrived(piece(i, c, part), z_send.at[i], z_recv.at[i, j], zp)

    def own(i):
        ring_send(i, ctx, 0, 0, zp)
        ring_send(i, ctx, 0, 4, zm)
        sib_send(i, ctx, 0)

    def hop(i, d):
        if d < 4:
            ring_got(i, minus(d), 0, d - 1)
            ring_send(i, minus(d), 0 if d < 3 else 1, d, zp)
            ring_got(i, plus(d), 0, 4 + d - 1)
            ring_send(i, plus(d), 0 if d < 3 else 2, 4 + d, zm)
            sib_send(i, minus(d), 2 * d - 1)
            sib_send(i, plus(d), 2 * d)
        else:
            ring_got(i, minus(4), 1, 3)
            ring_got(i, plus(4), 2, 7)
            sib_send(i, plus(4), 7)

    def sib_got(group, j):
        d = (j + 1) // 2
        pair = ctx + 1 - 2 * core
        c = lax.rem(pair + CTX - 2 * d, CTX) if j % 2 else lax.rem(pair + 2 * d, CTX)
        ref = kvt.at[c] if group == 0 else kvd.at[group - 1, c]
        arrived(ref, z_send.at[0], s_recv.at[group, j], sib)

    def ring_done(i):
        if i < N_T:
            _, r0, n = GATHERS[i]
            ref = kvt.at[pl.ds(0, 15), :, :, pl.ds(r0, n)]
        else:
            h, r0, n = PIECES[i - N_T]
            ref = kvd.at[h, pl.ds(0, 15), :, pl.ds(r0, n)]
        left(ref, z_send.at[i], z_recv.at[i, 0])

    def keys_values_t(g):
        _, r0, n = GATHERS[g]
        for h in range(HEADS_HERE):
            res = dot_nn(xg[0, pl.ds(r0, n), :], wbuf[:, pl.ds(h * LANES_KV, LANES_KV)]).astype(BF16)
            kvt[ctx, h, 0, pl.ds(r0, n), :] = res[:, :HD]
            kvt[ctx, h, 1, pl.ds(r0, n), :] = res[:, HD:]

    def keys_values_d(h):
        res = dot_nn(xg[1], wbuf[:, pl.ds(h * LANES_KV, LANES_KV)]).astype(BF16)
        kvd[h, ctx, 0] = res[:, :HD]
        kvd[h, ctx, 1] = res[:, HD:]

    def queries(a):
        res = dot_nn(xg[a], wbuf[:, pl.ds(3 * LANES_KV, COLS)]).astype(BF16)
        for h in range(HEADS_HERE):
            qcat[h, :, pl.ds((1 - a) * HD, HD)] = res[:, h * HD : (h + 1) * HD]

    ones = jnp.ones((2 * ROWS, HD), BF16)

    def wide(stat_rows):
        return jnp.concatenate([stat_rows] * (2 * ROWS // HD), axis=1)

    def attend(h, chip, first):
        c0 = chip * 2
        kk = kvt[pl.ds(c0, 2), h, 0].reshape(2 * ROWS, HD)
        vv = kvt[pl.ds(c0, 2), h, 1].reshape(2 * ROWS, HD)
        vcat = jnp.concatenate([vv, ones], axis=1)
        for blk in range(2):
            rows = pl.ds(blk * 128, 128)
            s = dot_nt(qcat[h, rows, pl.ds(HD, HD)], kk)
            top = jnp.broadcast_to(jnp.max(s, axis=1, keepdims=True), (128, HD))
            if not first:
                old = stat[h, 0, rows, :]
                top = jnp.maximum(old, top)
                keep = jnp.exp2((old - top) * (FACTOR * LOG2E))
            p = jnp.exp2((s - wide(top)) * (FACTOR * LOG2E)).astype(BF16)
            res = dot_nn(p, vcat)
            v_new, l_new = res[:, :HD], res[:, HD:]
            if not first:
                l_new += stat[h, 1, rows, :] * keep
                v_new += acc_v[h, rows, :] * keep
            stat[h, 0, rows, :] = top
            stat[h, 1, rows, :] = l_new
            acc_v[h, rows, :] = v_new

    def attend_dot(h, chip, first):
        c0 = chip * 2
        kk = kvt[pl.ds(c0, 2), h, 0].reshape(2 * ROWS, HD)
        vv = kvt[pl.ds(c0, 2), h, 1].reshape(2 * ROWS, HD)
        kd = kvd[h, pl.ds(c0, 2), 0].reshape(2 * ROWS, HD)
        vd = kvd[h, pl.ds(c0, 2), 1].reshape(2 * ROWS, HD)
        kcat = jnp.concatenate([kk, kd], axis=1)
        vcat = jnp.concatenate([vv, ones], axis=1)
        qq = qcat[h]
        s = dot_nt(qq[:, HD:], kk)
        sd = dot_nt(qq, kcat)
        p = jnp.exp2((s - wide(stat[h, 0])) * (FACTOR * LOG2E))
        res = dot_nn((p * sd).astype(BF16), vcat)
        w_new = res[:, :HD] * FACTOR + dot_nn(p.astype(BF16), vd)
        t_new = res[:, HD:]
        if not first:
            t_new += stat[h, 2]
            w_new += acc_w[h]
        stat[h, 2] = t_new
        acc_w[h] = w_new

    me_chip = ctx // 2

    def arrivals(d):
        return (0,) if d == 0 else ((2 * d - 1, 2 * d) if d < 4 else (7,))

    def chips(d):
        if d == 0:
            return (me_chip,)
        if d == 4:
            return (lax.rem(me_chip + 4, 8),)
        return (lax.rem(me_chip + 8 - d, 8), lax.rem(me_chip + d, 8))

    def t_got(d):
        for j in arrivals(d):
            sib_got(0, j)

    def d_got(h, d):
        for j in arrivals(d):
            sib_got(1 + h, j)

    def stage(d):
        for chip in chips(d):
            for h in range(HEADS_HERE):
                attend(h, chip, d == 0)

    def stage_dot(h, d):
        for chip in chips(d):
            attend_dot(h, chip, d == 0)

    def close():
        for h in range(HEADS_HERE):
            at[h, pl.ds(0, ROWS), cols(tp, HD)] = (acc_v[h] / stat[h, 1]).astype(BF16)

    def close_dot(h):
        l = stat[h, 1]
        res = (acc_w[h] - (stat[h, 2] * FACTOR / l) * acc_v[h]) / l
        at[h, pl.ds(ROWS, ROWS), cols(tp, HD)] = res.astype(BF16)

    def project():
        res = jnp.zeros((ROWS, COLS), F32)
        for h in range(HEADS_HERE):
            res += dot_nn(at[h, pl.ds(0, ROWS), :], wt[h].reshape(TP * HD, COLS))
        out_ref[...] = res.astype(BF16)

    def project_dot(h):
        res = dot_nn(at[h, pl.ds(ROWS, ROWS), :], wt[h].reshape(TP * HD, COLS))
        if h > 0:
            res += total[...]
        if h < HEADS_HERE - 1:
            total[...] = res
        else:
            outd_ref[...] = res.astype(BF16)

    def weights_send(j):
        send(
            wo.at[:, pl.ds(core * 64, 64), cols(slots[j], COLS)], wt.at[:, tp, core],
            p_send.at[0], p_recv.at[0], peers[j],
        )

    def weights_share():
        arrived(wt.at[:, pl.ds(0, 7), core], p_send.at[0], p_recv.at[0], xn)
        local[9].wait()
        send(wt.at[:, :, core], wt.at[:, :, core], p_send.at[1], p_recv.at[1], sib)

    def weights_got():
        arrived(wt.at[:, :, 1 - core], p_send.at[1], p_recv.at[1], sib)

    G = [acts(g) for g in range(len(GATHERS))]
    A = [heads_out(h) for h in range(HEADS_HERE + 1)]

    def make_t(g):
        G[g].finish()
        keys_values_t(g)

    def kvw_wait():
        for c in local[2:8]:
            c.wait()

    def d_gathered():
        for g in range(N_T, len(GATHERS)):
            G[g].finish()

    local[0].wait()
    G[0].start()
    G[1].start()
    G[2].start()
    kvw_wait()
    make_t(0)
    own(0)
    G[3].start()
    make_t(1)
    own(1)
    G[4].start()
    make_t(2)
    hop(0, 1)
    own(2)
    G[3].fwd(2)
    G[3].fwd(0)
    G[3].fwd(1)
    G[5].start()
    hop(1, 1)
    G[3].fwd(3)
    local[1].wait()
    G[6].start()
    G[4].fwd(0)
    G[4].fwd(1)
    hop(0, 2)
    G[4].fwd(2)
    hop(2, 1)
    G[4].fwd(3)
    G[5].fwd(1)
    G[5].fwd(0)
    hop(1, 2)
    make_t(3)
    own(3)
    G[5].fwd(3)
    G[5].fwd(2)
    G[7].start()
    hop(0, 3)
    G[6].fwd(1)
    G[6].fwd(0)
    hop(2, 2)
    G[6].fwd(2)
    make_t(4)
    hop(1, 3)
    own(4)
    make_t(5)
    own(5)
    G[6].fwd(3)
    local[8].wait()
    queries(0)
    hop(0, 4)
    hop(3, 1)
    G[8].start()
    hop(2, 3)
    t_got(0)
    stage(0)
    hop(1, 4)
    hop(4, 1)
    hop(5, 1)
    weights_send(0)
    hop(3, 2)
    t_got(1)
    stage(1)
    hop(2, 4)
    weights_send(1)
    weights_send(2)
    hop(4, 2)
    weights_send(3)
    hop(5, 2)
    d_gathered()
    keys_values_d(0)
    own(6)
    keys_values_d(1)
    own(7)
    keys_values_d(2)
    own(8)
    hop(3, 3)
    weights_send(4)
    queries(1)
    weights_send(5)
    hop(4, 3)
    hop(5, 3)
    d_got(0, 0)
    t_got(2)
    stage(2)
    hop(6, 1)
    d_got(1, 0)
    weights_send(6)
    t_got(3)
    stage(3)
    hop(7, 1)
    hop(8, 1)
    d_got(0, 1)
    hop(3, 4)
    hop(4, 4)
    hop(5, 4)
    d_got(1, 1)
    own(9)
    hop(6, 2)
    t_got(4)
    stage(4)
    hop(7, 2)
    close()
    A[3].start()
    stage_dot(1, 0)
    stage_dot(1, 1)
    own(10)
    weights_share()
    d_got(0, 2)
    stage_dot(0, 0)
    hop(8, 2)
    stage_dot(0, 1)
    hop(9, 1)
    stage_dot(0, 2)
    hop(6, 3)
    d_got(2, 0)
    stage_dot(2, 0)
    hop(7, 3)
    weights_got()
    d_got(1, 2)
    stage_dot(1, 2)
    hop(10, 1)
    d_got(0, 3)
    A[3].fwd(2)
    stage_dot(0, 3)
    d_got(2, 1)
    hop(8, 3)
    stage_dot(2, 1)
    A[3].fwd(0)
    hop(9, 2)
    A[3].fwd(3)
    hop(6, 4)
    A[3].fwd(1)
    hop(7, 4)
    d_got(1, 3)
    stage_dot(1, 3)
    hop(10, 2)
    d_got(0, 4)
    stage_dot(0, 4)
    close_dot(0)
    A[0].start()
    hop(8, 4)
    hop(9, 3)
    d_got(2, 2)
    stage_dot(2, 2)
    d_got(1, 4)
    stage_dot(1, 4)
    close_dot(1)
    A[1].start()
    hop(10, 3)
    hop(9, 4)
    A[3].finish()
    project()
    A[0].fwd(2)
    A[0].fwd(0)
    A[0].fwd(1)
    A[0].fwd(3)
    d_got(2, 3)
    stage_dot(2, 3)
    hop(10, 4)
    d_got(2, 4)
    stage_dot(2, 4)
    close_dot(2)
    A[2].start()
    A[1].finish()
    A[0].finish()
    project_dot(0)
    project_dot(1)
    A[2].finish()
    project_dot(2)
    for gather in G + A:
        gather.done()
    for i in range(N_ITEMS):
        ring_done(i)
    left(wt.at[:, pl.ds(0, 7), core], p_send.at[0], p_recv.at[0])
    left(wt.at[:, :, core], p_send.at[1], p_recv.at[1])


def hand_on(a_ref, b_ref, c_ref, d_ref):
    c_ref[...] = a_ref[...]
    d_ref[...] = b_ref[...]


def body(tokens, tangent, w_query, w_key, w_value, w_output):
    wo = w_output.reshape(HEADS_HERE, HD, D)
    hbm = pl.BlockSpec(memory_space=pl.ANY)
    vmem = pl.BlockSpec(memory_space=pltpu.VMEM)
    dma = pltpu.SemaphoreType.DMA
    n_g = len(GATHERS)
    layer_out, layer_tangent = pl.pallas_call(
        kernel,
        out_shape=[jax.ShapeDtypeStruct((ROWS, COLS), BF16)] * 2,
        in_specs=[hbm] * 6,
        out_specs=[vmem] * 2,
        scratch_shapes=[
            pltpu.VMEM((2, ROWS, D), BF16),
            pltpu.VMEM((D, 3 * COLS), BF16),
            pltpu.VMEM((CTX, HEADS_HERE, 2, ROWS, HD), BF16),
            pltpu.VMEM((HEADS_HERE, CTX, 2, ROWS, HD), BF16),
            pltpu.VMEM((HEADS_HERE, ROWS, 2 * HD), BF16),
            pltpu.VMEM((HEADS_HERE, TP, 2, 64, COLS), BF16),
            pltpu.VMEM((HEADS_HERE, 2 * ROWS, TP * HD), BF16),
            pltpu.VMEM((HEADS_HERE, ROWS, HD), F32),
            pltpu.VMEM((HEADS_HERE, ROWS, HD), F32),
            pltpu.VMEM((HEADS_HERE, 3, ROWS, HD), F32),
            pltpu.VMEM((ROWS, COLS), F32),
            dma((10,)),
            dma((n_g, 9)),
            dma((n_g, 9)),
            dma((N_ITEMS,)),
            dma((N_ITEMS, 8)),
            dma((1 + HEADS_HERE, 8)),
            dma((HEADS_HERE + 1, 9)),
            dma((HEADS_HERE + 1, 9)),
            dma((2,)),
            dma((2,)),
        ],
        compiler_params=pltpu.CompilerParams(
            collective_id=0, has_side_effects=True, vmem_limit_bytes=56 << 20
        ),
        cost_estimate=pl.CostEstimate(flops=12_000_000_000, bytes_accessed=40_000_000, transcendentals=3_200_000),
    )(tokens, tangent, w_query, w_key, w_value, wo)
    return tuple(
        pl.pallas_call(
            hand_on,
            out_shape=[jax.ShapeDtypeStruct((ROWS, COLS), BF16)] * 2,
            in_specs=[vmem] * 2,
            out_specs=[vmem] * 2,
        )(layer_out, layer_tangent)
    )


def solution(mesh):
    placed = (
        P(("dp", "ctx"), "tp"),
        P(("dp", "ctx"), "tp"),
        P(None, "tp"),
        P(None, "tp"),
        P(None, "tp"),
        P("tp", None),
    )
    return jax.shard_map(
        body,
        mesh=mesh,
        in_specs=placed,
        out_specs=(P(("dp", "ctx"), "tp"), P(("dp", "ctx"), "tp")),
        check_vma=False,
    )
```

```python
import jax
import jax.numpy as jnp
from jax import lax
from jax.experimental import pallas as pl
from jax.experimental.pallas import tpu as pltpu
from jax.sharding import PartitionSpec as P

MESH = pl.DeviceIdType.MESH
HD = 128
HEADS_HERE = 3
ROWS = 256
COLS = 384
D = 3072
CTX = 16
TP = 8
LANES_KV = 2 * HD
FACTOR = HD ** (-0.5)
LOG2E = 1.4426950408889634
BF16 = jnp.bfloat16
F32 = jnp.float32

GATHERS = ((0, 0, 32), (0, 32, 32), (0, 64, 32), (0, 96, 64), (0, 160, 64), (0, 224, 32), (1, 0, 256))
DIRECT = (True, True, True, True, True, True, False)
DIRECT_OUT = (False, True, True, False)
N_T = 6
PIECES = ((0, 0, 128), (0, 128, 128), (1, 0, 192), (1, 192, 64), (2, 0, 192), (2, 192, 64))
N_ITEMS = N_T + len(PIECES)


def dot_nt(a, b):
    return lax.dot_general(a, b, (((1,), (1,)), ((), ())), preferred_element_type=F32)


def dot_nn(a, b):
    return jnp.dot(a, b, preferred_element_type=F32)


def kernel(
    tok, tan, wq, wk, wv, wo, out_ref, outd_ref,
    xg, wbuf, kvt, kvd, qcat, wt, at, acc_v, acc_w, stat, total,
    loc_sem, g_send, g_recv, z_send, z_recv, s_recv, a_send, a_recv, p_send, p_recv,
):
    dp, ctx, tp = lax.axis_index("dp"), lax.axis_index("ctx"), lax.axis_index("tp")
    core = lax.rem(ctx, 2)
    x, y = tp // 4, lax.rem(tp, 4)
    y_up, y_down, y_far = lax.rem(y + 1, 4), lax.rem(y + 3, 4), lax.rem(y + 2, 4)
    other = 1 - x
    zp = (dp, lax.rem(ctx + 2, CTX), tp)
    zm = (dp, lax.rem(ctx + 14, CTX), tp)
    sib = (dp, ctx + 1 - 2 * core, tp)

    def plane(xx, yy):
        return (dp, ctx, xx * 4 + yy)

    xn, yp, ym = plane(other, y), plane(x, y_up), plane(x, y_down)
    xyp, xym = plane(other, y_up), plane(other, y_down)
    s_x, s_p, s_m = other * 4 + y, x * 4 + y_up, x * 4 + y_down
    s_xp, s_xm = other * 4 + y_up, other * 4 + y_down
    s_f, s_xf = x * 4 + y_far, other * 4 + y_far
    peers = (xn, yp, ym, xyp, xym, plane(x, y_far), plane(other, y_far))

    slots = (s_x, s_p, s_m, s_xp, s_xm, s_f, s_xf)
    back = (s_x, s_m, s_p, s_xm, s_xp, s_f, s_xf)

    def cols(slot, width):
        return pl.ds(pl.multiple_of(slot * width, 128), width)

    local = [
        pltpu.make_async_copy(tok, xg.at[0, :, cols(tp, COLS)], loc_sem.at[0]),
        pltpu.make_async_copy(tan, xg.at[1, :, cols(tp, COLS)], loc_sem.at[1]),
    ]
    for h in range(HEADS_HERE):
        for j, w in enumerate((wk, wv)):
            local.append(
                pltpu.make_async_copy(
                    w.at[:, pl.ds(h * HD, HD)],
                    wbuf.at[:, pl.ds(h * LANES_KV + j * HD, HD)],
                    loc_sem.at[2 + 2 * h + j],
                )
            )
    local.append(
        pltpu.make_async_copy(wq, wbuf.at[:, pl.ds(3 * LANES_KV, COLS)], loc_sem.at[8])
    )
    local.append(
        pltpu.make_async_copy(
            wo.at[:, pl.ds(core * 64, 64), cols(tp, COLS)], wt.at[:, tp, core], loc_sem.at[9]
        )
    )
    for c in local:
        c.start()

    barrier = pltpu.get_barrier_semaphore()
    greet = (zp, zm, sib) + peers
    for dev in greet:
        pl.semaphore_signal(barrier, inc=1, device_id=dev, device_id_type=MESH)
    pl.semaphore_wait(barrier, len(greet))

    def send(src, dst, ssem, rsem, dev):
        pltpu.make_async_remote_copy(
            src_ref=src, dst_ref=dst, send_sem=ssem, recv_sem=rsem, device_id=dev, device_id_type=MESH
        ).start()

    def left(ref, ssem, rsem):
        pltpu.make_async_remote_copy(
            src_ref=ref, dst_ref=ref, send_sem=ssem, recv_sem=rsem, device_id=xn, device_id_type=MESH
        ).wait_send()

    def arrived(ref, ssem, rsem, dev):
        pltpu.make_async_remote_copy(
            src_ref=ref, dst_ref=ref, send_sem=ssem, recv_sem=rsem, device_id=dev, device_id_type=MESH
        ).wait_recv()

    class Gather:
        def __init__(self, view, blocks, ssem, rsem, n, direct):
            self.view, self.blocks, self.n, self.direct = view, blocks, n, direct
            self.ssem, self.rsem = ssem, rsem

        def part(self, slot, part):
            half = self.n // 2
            lo, n = ((0, self.n), (0, half), (half, half))[part]
            return self.view(slot, lo, n)

        def go(self, slot, part, j, dev):
            ref = self.part(slot, part)
            send(ref, ref, self.ssem(0), self.rsem(j), dev)

        def start(self):
            for j in (6, 5, 3, 4, 0, 1, 2) if self.direct else (3, 4, 1, 2, 0):
                self.go(tp, 0, 0 if self.direct else j, peers[j])

        def fwd(self, k):
            arrived(self.part(back[1 + k], 0), self.ssem(0), self.rsem(1 + k), xn)
            self.go(back[1 + k], 1 + k % 2, 0, (yp, ym)[k % 2])

        def finish(self):
            arrived(self.blocks(7 if self.direct else 3), self.ssem(0), self.rsem(0), xn)

        def done(self):
            left(self.blocks(7), self.ssem(0), self.rsem(0))

    def acts(g):
        a, r0, n = GATHERS[g]
        return Gather(
            lambda slot, lo, cnt: xg.at[a, pl.ds(r0 + lo, cnt), cols(slot, COLS)],
            lambda cnt: xg.at[a, pl.ds(r0, n), pl.ds(0, cnt * COLS)],
            lambda j: g_send.at[g, j], lambda j: g_recv.at[g, j], n, DIRECT[g],
        )

    def heads_out(h):
        if h < HEADS_HERE:
            view = lambda slot, lo, cnt: at.at[h, pl.ds(ROWS + lo, cnt), cols(slot, HD)]
            blocks = lambda cnt: at.at[h, pl.ds(ROWS, ROWS), pl.ds(0, cnt * HD)]
        else:
            view = lambda slot, lo, cnt: at.at[:, pl.ds(lo, cnt), cols(slot, HD)]
            blocks = lambda cnt: at.at[:, pl.ds(0, ROWS), pl.ds(0, cnt * HD)]
        return Gather(view, blocks, lambda j: a_send.at[h, j], lambda j: a_recv.at[h, j], ROWS, DIRECT_OUT[h])

    def piece(i, c, part):
        if i < N_T:
            _, r0, n = GATHERS[i]
            if part == 0:
                return kvt.at[c, :, :, pl.ds(r0, n)]
            return kvt.at[c, :, part - 1, pl.ds(r0, n)]
        h, r0, n = PIECES[i - N_T]
        if part == 0:
            return kvd.at[h, c, :, pl.ds(r0, n)]
        return kvd.at[h, c, part - 1, pl.ds(r0, n)]

    def minus(d):
        return lax.rem(ctx + CTX - 2 * d, CTX)

    def plus(d):
        return lax.rem(ctx + 2 * d, CTX)

    def ring_send(i, c, part, j, dev):
        ref = piece(i, c, part)
        send(ref, ref, z_send.at[i], z_recv.at[i, j], dev)

    def shared(i):
        return 0 if i < N_T else 1 + PIECES[i - N_T][0]

    def sib_send(i, c, j):
        ref = piece(i, c, 0)
        send(ref, ref, z_send.at[i], s_recv.at[shared(i), j], sib)

    def ring_got(i, c, part, j):
        arrived(piece(i, c, part), z_send.at[i], z_recv.at[i, j], zp)

    def own(i):
        ring_send(i, ctx, 0, 0, zp)
        ring_send(i, ctx, 0, 4, zm)
        sib_send(i, ctx, 0)

    def hop(i, d):
        if d < 4:
            ring_got(i, minus(d), 0, d - 1)
            ring_send(i, minus(d), 0 if d < 3 else 1, d, zp)
            ring_got(i, plus(d), 0, 4 + d - 1)
            ring_send(i, plus(d), 0 if d < 3 else 2, 4 + d, zm)
            sib_send(i, minus(d), 2 * d - 1)
            sib_send(i, plus(d), 2 * d)
        else:
            ring_got(i, minus(4), 1, 3)
            ring_got(i, plus(4), 2, 7)
            sib_send(i, plus(4), 7)

    def sib_got(group, j):
        d = (j + 1) // 2
        pair = ctx + 1 - 2 * core
        c = lax.rem(pair + CTX - 2 * d, CTX) if j % 2 else lax.rem(pair + 2 * d, CTX)
        ref = kvt.at[c] if group == 0 else kvd.at[group - 1, c]
        arrived(ref, z_send.at[0], s_recv.at[group, j], sib)

    def ring_done(i):
        if i < N_T:
            _, r0, n = GATHERS[i]
            ref = kvt.at[pl.ds(0, 15), :, :, pl.ds(r0, n)]
        else:
            h, r0, n = PIECES[i - N_T]
            ref = kvd.at[h, pl.ds(0, 15), :, pl.ds(r0, n)]
        left(ref, z_send.at[i], z_recv.at[i, 0])

    def keys_values_t(g):
        _, r0, n = GATHERS[g]
        for h in range(HEADS_HERE):
            res = dot_nn(xg[0, pl.ds(r0, n), :], wbuf[:, pl.ds(h * LANES_KV, LANES_KV)]).astype(BF16)
            kvt[ctx, h, 0, pl.ds(r0, n), :] = res[:, :HD]
            kvt[ctx, h, 1, pl.ds(r0, n), :] = res[:, HD:]

    def keys_values_d(h):
        res = dot_nn(xg[1], wbuf[:, pl.ds(h * LANES_KV, LANES_KV)]).astype(BF16)
        kvd[h, ctx, 0] = res[:, :HD]
        kvd[h, ctx, 1] = res[:, HD:]

    def queries(a):
        res = dot_nn(xg[a], wbuf[:, pl.ds(3 * LANES_KV, COLS)]).astype(BF16)
        for h in range(HEADS_HERE):
            qcat[h, :, pl.ds((1 - a) * HD, HD)] = res[:, h * HD : (h + 1) * HD]

    ones = jnp.ones((2 * ROWS, HD), BF16)

    def wide(stat_rows):
        return jnp.concatenate([stat_rows] * (2 * ROWS // HD), axis=1)

    def attend(h, chip, first):
        c0 = chip * 2
        kk = kvt[pl.ds(c0, 2), h, 0].reshape(2 * ROWS, HD)
        vv = kvt[pl.ds(c0, 2), h, 1].reshape(2 * ROWS, HD)
        vcat = jnp.concatenate([vv, ones], axis=1)
        for blk in range(2):
            rows = pl.ds(blk * 128, 128)
            s = dot_nt(qcat[h, rows, pl.ds(HD, HD)], kk)
            top = jnp.broadcast_to(jnp.max(s, axis=1, keepdims=True), (128, HD))
            if not first:
                old = stat[h, 0, rows, :]
                top = jnp.maximum(old, top)
                keep = jnp.exp2((old - top) * (FACTOR * LOG2E))
            p = jnp.exp2((s - wide(top)) * (FACTOR * LOG2E)).astype(BF16)
            res = dot_nn(p, vcat)
            v_new, l_new = res[:, :HD], res[:, HD:]
            if not first:
                l_new += stat[h, 1, rows, :] * keep
                v_new += acc_v[h, rows, :] * keep
            stat[h, 0, rows, :] = top
            stat[h, 1, rows, :] = l_new
            acc_v[h, rows, :] = v_new

    def attend_dot(h, chip, first):
        c0 = chip * 2
        kk = kvt[pl.ds(c0, 2), h, 0].reshape(2 * ROWS, HD)
        vv = kvt[pl.ds(c0, 2), h, 1].reshape(2 * ROWS, HD)
        kd = kvd[h, pl.ds(c0, 2), 0].reshape(2 * ROWS, HD)
        vd = kvd[h, pl.ds(c0, 2), 1].reshape(2 * ROWS, HD)
        kcat = jnp.concatenate([kk, kd], axis=1)
        vcat = jnp.concatenate([vv, ones], axis=1)
        qq = qcat[h]
        s = dot_nt(qq[:, HD:], kk)
        sd = dot_nt(qq, kcat)
        p = jnp.exp2((s - wide(stat[h, 0])) * (FACTOR * LOG2E))
        res = dot_nn((p * sd).astype(BF16), vcat)
        w_new = res[:, :HD] * FACTOR + dot_nn(p.astype(BF16), vd)
        t_new = res[:, HD:]
        if not first:
            t_new += stat[h, 2]
            w_new += acc_w[h]
        stat[h, 2] = t_new
        acc_w[h] = w_new

    me_chip = ctx // 2

    def arrivals(d):
        return (0,) if d == 0 else ((2 * d - 1, 2 * d) if d < 4 else (7,))

    def chips(d):
        if d == 0:
            return (me_chip,)
        if d == 4:
            return (lax.rem(me_chip + 4, 8),)
        return (lax.rem(me_chip + 8 - d, 8), lax.rem(me_chip + d, 8))

    def t_got(d):
        for j in arrivals(d):
            sib_got(0, j)

    def d_got(h, d):
        for j in arrivals(d):
            sib_got(1 + h, j)

    def stage(d):
        for chip in chips(d):
            for h in range(HEADS_HERE):
                attend(h, chip, d == 0)

    def stage_dot(h, d):
        for chip in chips(d):
            attend_dot(h, chip, d == 0)

    def close():
        for h in range(HEADS_HERE):
            at[h, pl.ds(0, ROWS), cols(tp, HD)] = (acc_v[h] / stat[h, 1]).astype(BF16)

    def close_dot(h):
        l = stat[h, 1]
        res = (acc_w[h] - (stat[h, 2] * FACTOR / l) * acc_v[h]) / l
        at[h, pl.ds(ROWS, ROWS), cols(tp, HD)] = res.astype(BF16)

    def project():
        res = jnp.zeros((ROWS, COLS), F32)
        for h in range(HEADS_HERE):
            res += dot_nn(at[h, pl.ds(0, ROWS), :], wt[h].reshape(TP * HD, COLS))
        out_ref[...] = res.astype(BF16)

    def project_dot(h):
        res = dot_nn(at[h, pl.ds(ROWS, ROWS), :], wt[h].reshape(TP * HD, COLS))
        if h > 0:
            res += total[...]
        if h < HEADS_HERE - 1:
            total[...] = res
        else:
            outd_ref[...] = res.astype(BF16)

    def weights_send(j):
        send(
            wo.at[:, pl.ds(core * 64, 64), cols(slots[j], COLS)], wt.at[:, tp, core],
            p_send.at[0], p_recv.at[0], peers[j],
        )

    def weights_share():
        arrived(wt.at[:, pl.ds(0, 7), core], p_send.at[0], p_recv.at[0], xn)
        local[9].wait()
        send(wt.at[:, :, core], wt.at[:, :, core], p_send.at[1], p_recv.at[1], sib)

    def weights_got():
        arrived(wt.at[:, :, 1 - core], p_send.at[1], p_recv.at[1], sib)

    G = [acts(g) for g in range(len(GATHERS))]
    A = [heads_out(h) for h in range(HEADS_HERE + 1)]

    def make_t(g):
        G[g].finish()
        keys_values_t(g)

    def kvw_wait():
        for c in local[2:8]:
            c.wait()

    def d_gathered():
        for g in range(N_T, len(GATHERS)):
            G[g].finish()

    def sent_earlier():
        for gather in G + [A[0], A[1], A[3]]:
            gather.done()
        for i in range(N_ITEMS):
            ring_done(i)
        left(wt.at[:, pl.ds(0, 7), core], p_send.at[0], p_recv.at[0])
        left(wt.at[:, :, core], p_send.at[1], p_recv.at[1])

    local[0].wait()
    G[0].start()
    G[1].start()
    G[2].start()
    G[3].start()
    kvw_wait()
    make_t(0)
    own(0)
    G[4].start()
    make_t(1)
    own(1)
    hop(0, 1)
    make_t(2)
    own(2)
    G[5].start()
    hop(1, 1)
    hop(0, 2)
    local[1].wait()
    G[6].start()
    hop(2, 1)
    make_t(3)
    hop(1, 2)
    own(3)
    hop(0, 3)
    hop(2, 2)
    hop(1, 3)
    make_t(4)
    own(4)
    hop(3, 1)
    make_t(5)
    own(5)
    local[8].wait()
    queries(0)
    hop(2, 3)
    hop(1, 4)
    t_got(0)
    hop(0, 4)
    stage(0)
    hop(4, 1)
    G[6].fwd(2)
    hop(3, 2)
    weights_send(0)
    hop(5, 1)
    hop(2, 4)
    G[6].fwd(1)
    G[6].fwd(0)
    t_got(1)
    G[6].fwd(3)
    stage(1)
    hop(4, 2)
    weights_send(1)
    weights_send(2)
    hop(3, 3)
    weights_send(3)
    hop(5, 2)
    weights_send(4)
    d_gathered()
    keys_values_d(0)
    own(6)
    own(7)
    keys_values_d(1)
    hop(3, 4)
    queries(1)
    hop(5, 3)
    t_got(2)
    hop(4, 3)
    keys_values_d(2)
    hop(6, 1)
    stage(2)
    hop(7, 1)
    hop(5, 4)
    own(8)
    d_got(0, 0)
    hop(4, 4)
    weights_send(5)
    weights_send(6)
    t_got(3)
    stage(3)
    d_got(0, 1)
    own(9)
    hop(6, 2)
    hop(7, 2)
    t_got(4)
    stage(4)
    close()
    A[3].start()
    d_got(0, 2)
    hop(8, 1)
    d_got(1, 0)
    stage_dot(1, 0)
    hop(9, 1)
    stage_dot(0, 0)
    stage_dot(0, 1)
    hop(6, 3)
    stage_dot(0, 2)
    hop(7, 3)
    d_got(1, 1)
    stage_dot(1, 1)
    own(10)
    weights_share()
    hop(8, 2)
    d_got(0, 3)
    stage_dot(0, 3)
    hop(9, 2)
    hop(6, 4)
    hop(7, 4)
    A[3].fwd(2)
    weights_got()
    own(11)
    d_got(1, 2)
    hop(10, 1)
    d_got(0, 4)
    A[3].fwd(3)
    stage_dot(0, 4)
    d_got(2, 0)
    close_dot(0)
    A[0].start()
    stage_dot(2, 0)
    hop(8, 3)
    A[3].fwd(0)
    hop(9, 3)
    A[3].fwd(1)
    hop(11, 1)
    stage_dot(1, 2)
    d_got(1, 3)
    stage_dot(1, 3)
    hop(10, 2)
    d_got(2, 1)
    stage_dot(2, 1)
    hop(8, 4)
    A[0].fwd(0)
    A[0].fwd(1)
    hop(9, 4)
    hop(11, 2)
    A[0].fwd(3)
    A[0].fwd(2)
    d_got(1, 4)
    stage_dot(1, 4)
    close_dot(1)
    hop(10, 3)
    A[1].start()
    hop(11, 3)
    d_got(2, 2)
    stage_dot(2, 2)
    A[3].finish()
    project()
    d_got(2, 3)
    hop(10, 4)
    hop(11, 4)
    stage_dot(2, 3)
    A[0].finish()
    project_dot(0)
    d_got(2, 4)
    stage_dot(2, 4)
    close_dot(2)
    A[2].start()
    A[1].finish()
    project_dot(1)
    sent_earlier()
    A[2].finish()
    project_dot(2)
    A[2].done()


def hand_on(a_ref, b_ref, c_ref, d_ref):
    c_ref[...] = a_ref[...]
    d_ref[...] = b_ref[...]


def body(tokens, tangent, w_query, w_key, w_value, w_output):
    wo = w_output.reshape(HEADS_HERE, HD, D)
    hbm = pl.BlockSpec(memory_space=pl.ANY)
    vmem = pl.BlockSpec(memory_space=pltpu.VMEM)
    dma = pltpu.SemaphoreType.DMA
    n_g = len(GATHERS)
    layer_out, layer_tangent = pl.pallas_call(
        kernel,
        out_shape=[jax.ShapeDtypeStruct((ROWS, COLS), BF16)] * 2,
        in_specs=[hbm] * 6,
        out_specs=[vmem] * 2,
        scratch_shapes=[
            pltpu.VMEM((2, ROWS, D), BF16),
            pltpu.VMEM((D, 3 * COLS), BF16),
            pltpu.VMEM((CTX, HEADS_HERE, 2, ROWS, HD), BF16),
            pltpu.VMEM((HEADS_HERE, CTX, 2, ROWS, HD), BF16),
            pltpu.VMEM((HEADS_HERE, ROWS, 2 * HD), BF16),
            pltpu.VMEM((HEADS_HERE, TP, 2, 64, COLS), BF16),
            pltpu.VMEM((HEADS_HERE, 2 * ROWS, TP * HD), BF16),
            pltpu.VMEM((HEADS_HERE, ROWS, HD), F32),
            pltpu.VMEM((HEADS_HERE, ROWS, HD), F32),
            pltpu.VMEM((HEADS_HERE, 3, ROWS, HD), F32),
            pltpu.VMEM((ROWS, COLS), F32),
            dma((10,)),
            dma((n_g, 9)),
            dma((n_g, 9)),
            dma((N_ITEMS,)),
            dma((N_ITEMS, 8)),
            dma((1 + HEADS_HERE, 8)),
            dma((HEADS_HERE + 1, 9)),
            dma((HEADS_HERE + 1, 9)),
            dma((2,)),
            dma((2,)),
        ],
        compiler_params=pltpu.CompilerParams(
            collective_id=0, has_side_effects=True, vmem_limit_bytes=56 << 20
        ),
        cost_estimate=pl.CostEstimate(flops=12_000_000_000, bytes_accessed=40_000_000, transcendentals=3_200_000),
    )(tokens, tangent, w_query, w_key, w_value, wo)
    return tuple(
        pl.pallas_call(
            hand_on,
            out_shape=[jax.ShapeDtypeStruct((ROWS, COLS), BF16)] * 2,
            in_specs=[vmem] * 2,
            out_specs=[vmem] * 2,
        )(layer_out, layer_tangent)
    )


def solution(mesh):
    placed = (
        P(("dp", "ctx"), "tp"),
        P(("dp", "ctx"), "tp"),
        P(None, "tp"),
        P(None, "tp"),
        P(None, "tp"),
        P("tp", None),
    )
    return jax.shard_map(
        body,
        mesh=mesh,
        in_specs=placed,
        out_specs=(P(("dp", "ctx"), "tp"), P(("dp", "ctx"), "tp")),
        check_vma=False,
    )
```
